32 devices in a mesh: seq: 2 (over x), shard: 16 (over z, y, core).
Axes of the slice: x: 2, y: 2, z: 4, core: 2. Of those that a mesh axis runs over, the one named last changes fastest.
Arguments:
- tokens_in: bfloat16 [16, 256, 768], P('shard', 'seq'), may hold values from -6 to 6
- w_query: bfloat16 [768, 768], P(('seq', 'shard')), may hold values from -0.02734375 to 0.02734375
- w_key: bfloat16 [768, 768], P(('seq', 'shard')), may hold values from -0.21875 to 0.21875
- w_value: bfloat16 [768, 768], P(('seq', 'shard')), may hold values from -0.21875 to 0.21875
- output_weight: bfloat16 [768, 768], P(('seq', 'shard')), may hold values from -1.25 to 1.25
- gain_attn: bfloat16 [768], P(('seq', 'shard')), may hold values from 0.25 to 1.75
- gain_moe: bfloat16 [768], P(('seq', 'shard')), may hold values from 0.25 to 1.75
- router_weight: bfloat16 [768, 8], P(('seq', 'shard')), may hold values from -0.16210938 to 0.16210938
- bias_table: bfloat16 [12, 32], P('seq'), may hold values from -4 to 4
- w_expert_in: bfloat16 [16, 768, 1536], P('shard'), may hold values from -0.21875 to 0.21875
- w_expert_out: bfloat16 [16, 1536, 768], P('shard'), may hold values from -0.4375 to 0.4375
- expert_id: int32 [16, 256], P('shard', 'seq'), may hold values from 0 to 7, as said below
- slot_id: int32 [16, 256], P('shard', 'seq'), may hold values from -1 to 19, as said below
- bucket_id: int32 [511], replicated, may hold values from 0 to 31
- cotangent: bfloat16 [16, 256, 768], P('shard', 'seq'), may hold values from -6 to 6
Outputs:
- block_out: bfloat16 [16, 256, 768], P('shard', 'seq')
- grad_tokens: float32 [16, 256, 768], P('shard', 'seq')
- grad_query: float32 [768, 768], P(('seq', 'shard'))
- grad_key: float32 [768, 768], P(('seq', 'shard'))
- grad_value: float32 [768, 768], P(('seq', 'shard'))
- grad_output: float32 [768, 768], P(('seq', 'shard'))
- grad_gain_attn: float32 [768], P(('seq', 'shard'))
- grad_gain_moe: float32 [768], P(('seq', 'shard'))
- grad_router: float32 [768, 8], P(('seq', 'shard'))
- grad_table: float32 [12, 32], P('seq')
- grad_expert_in: float32 [16, 768, 1536], P('shard', None, 'seq')
- grad_expert_out: float32 [16, 1536, 768], P('shard', 'seq')
The draws below stay inside these ranges and needn't reach their ends.
Inputs may be any that keep to these rules, and one draw needn't show every extreme that they name: `expert_id`: in every aligned block of 128 positions of one sequence some expert is named by more than 20 tokens. `slot_id`: a token's slot is its rank, from 0 in position order, among the tokens of its aligned block of 128 positions that name the same expert; -1 where that rank is 20 or more.
All inputs are finite; a program needn't handle non-finite values.
Results may differ from the reference program's by a relative error of at most 0.014.
Values may be sent and summed in bfloat16 or wider, within the bound.
A program may use at most 128 MiB of HBM per device.

```python
import jax
import jax.numpy as jnp
from jax import lax

D = 768
HEADS = 12
HEAD_DIM = 64
FF = 3072
BUCKETS = 32
TOK_DEV = 128
LEN = 256
SEQS = 16
EXPERTS = 8
CAP = 20
N_SEQ = 2


def routing_tables(key):
    blocks = SEQS * (LEN // TOK_DEV)
    keys = jax.random.split(key, 6)
    first = jax.random.randint(keys[0], (blocks, TOK_DEV), 0, EXPERTS)
    second = jax.random.randint(keys[1], (blocks, TOK_DEV), 0, EXPERTS)
    coin = jax.random.randint(keys[2], (blocks, TOK_DEV), 0, 2)
    ranked = jnp.where(coin == 1, first * second // EXPERTS, first)
    relabel = jax.random.permutation(keys[3], EXPERTS)
    chosen = relabel[ranked]
    busiest = jax.random.randint(keys[4], (blocks, 1), 0, EXPERTS)
    orders = jax.vmap(lambda sub: jax.random.permutation(sub, TOK_DEV))(jax.random.split(keys[5], blocks))
    chosen = jnp.where(orders <= CAP, busiest, chosen).astype(jnp.int32)
    table = (chosen[:, :, None] == jnp.arange(EXPERTS, dtype=jnp.int32)[None, None, :]).astype(jnp.int32)
    earlier = jnp.cumsum(table, axis=1) - table
    ranks = jnp.sum(earlier * table, axis=2)
    slots = jnp.where(ranks < CAP, ranks, -1).astype(jnp.int32)
    return (chosen.reshape(SEQS, LEN), slots.reshape(SEQS, LEN))


def draw_expert_id(key, part):
    shared = routing_tables(key)
    return shared[0]


def draw_slot_id(key, part):
    shared = routing_tables(key)
    return shared[1]


def set_ends(result, own_key, smallest, largest):
    longest = result.shape.index(max(result.shape))
    spots = []
    for shift in (0, 1):
        where = [jax.random.randint(jax.random.fold_in(own_key, axis), (), 0, length) for axis, length in enumerate(result.shape)]
        where[longest] = (where[longest] + shift) % result.shape[longest]
        spots.append(tuple(where))
    return result.at[spots[0]].set(smallest).at[spots[1]].set(largest)


def steps_of(own_key, dims, shards, least, largest):
    def one(position, shards_of):
        draws = jax.random.uniform(jax.random.fold_in(jax.random.fold_in(own_key, 6), position), (shards_of,), jnp.float32, least / len(shards), largest / len(shards))
        return jnp.repeat(jnp.exp(draws), dims[position] // shards_of).reshape((-1,) + (1,) * (len(dims) - position - 1))

    factor_of = one(*shards[0])
    for cut in shards[1:]:
        factor_of = factor_of * one(*cut)
    return factor_of


def gaussian(stream_key, shape, width, bound, cuts=(), held_as=jnp.bfloat16):
    array = width * jax.random.normal(stream_key, shape, jnp.float32)
    if cuts:
        array = array * steps_of(stream_key, shape, cuts, -0.22, 0.18)
    return jnp.clip(array, -bound, bound).astype(held_as)


def setup_inputs(seed: int = 0) -> dict:
    seeds = jax.random.split(jax.random.key(seed), 16)
    return {
        "tokens_in": gaussian(seeds[0], (SEQS, LEN, D), 1.0, 6.0, ((0, 16), (1, 2))),
        "w_query": gaussian(seeds[1], (D, D), (D * HEAD_DIM) ** -0.5, 0.02734375, ((0, 32),)),
        "w_key": gaussian(seeds[2], (D, D), D ** -0.5, 0.21875, ((0, 32),)),
        "w_value": gaussian(seeds[3], (D, D), D ** -0.5, 0.21875, ((0, 32),)),
        "output_weight": gaussian(seeds[4], (D, D), (D * 8 / LEN) ** -0.5, 1.25, ((0, 32),)),
        "gain_attn": jnp.clip(1.0 + 0.15 * jax.random.normal(seeds[5], (D,), jnp.float32), 0.25, 1.75).astype(jnp.bfloat16),
        "gain_moe": jnp.clip(1.0 + 0.15 * jax.random.normal(seeds[6], (D,), jnp.float32), 0.25, 1.75).astype(jnp.bfloat16),
        "router_weight": gaussian(seeds[7], (D, EXPERTS), (0.75 / D ** 0.5), 0.16210938, ((0, 32),)),
        "bias_table": gaussian(seeds[8], (HEADS, BUCKETS), 1.0, 4.0, ((0, 2),)),
        "w_expert_in": gaussian(seeds[9], (2 * EXPERTS, D, FF // 2), D ** -0.5, 0.21875, ((0, 16),)),
        "w_expert_out": gaussian(seeds[10], (2 * EXPERTS, FF // 2, D), (FF / (2 * EXPERTS)) ** -0.5, 0.4375, ((0, 16),)),
        "expert_id": draw_expert_id(jax.random.fold_in(seeds[15], 71), 0),
        "slot_id": draw_slot_id(jax.random.fold_in(seeds[15], 71), 0),
        "bucket_id": set_ends(jax.random.randint(seeds[13], (2 * LEN - 1,), 0, BUCKETS), jax.random.fold_in(seeds[13], 1), 0, BUCKETS - 1).astype(jnp.int32),
        "cotangent": gaussian(seeds[14], (SEQS, LEN, D), 1.0, 6.0, ((0, 16), (1, 2))),
    }


EPS = 1e-06
TOP_PRECISION = lax.Precision.HIGHEST

@jax.custom_vjp
def low(v):
    return lax.optimization_barrier(v.astype(jnp.bfloat16)).astype(jnp.float32)

@jax.custom_vjp
def reduced_backward(v):
    return v

def low_keep(v):
    return (low(v), None)

def low_pass(kept, grad):
    return (grad,)

def back_keep(v):
    return (v, None)

def back_low(kept, grad):
    return (low(grad),)
low.defvjp(low_keep, low_pass)
reduced_backward.defvjp(back_keep, back_low)

def normalize(values, gain):
    inverse = lax.rsqrt(lax.optimization_barrier(jnp.mean(values * values, axis=-1, keepdims=True)) + EPS)
    return values * inverse * gain

def softmax_rows(scores):
    row_top = lax.optimization_barrier(jnp.max(scores, axis=-1, keepdims=True))
    weights = jnp.exp(scores - row_top)
    return weights / lax.optimization_barrier(jnp.sum(weights, axis=-1, keepdims=True))

def attention(queries, key_heads, value_heads, bias):
    scores = jnp.einsum('gqhd,gkhd->ghqk', queries, key_heads, precision=TOP_PRECISION) + bias[None]
    scores = reduced_backward(scores)
    probs_low = low(softmax_rows(scores))
    mixed_heads = jnp.einsum('ghqk,gkhd->gqhd', probs_low, value_heads, precision=TOP_PRECISION)
    return reduced_backward(low(mixed_heads))

def forward(tokens, w_query, w_key, w_value, output_weight, gain_attn, gain_moe, router_weight, bias_table, w_expert_in, w_expert_out, expert_id, slot_id, bucket_id):
    sequences, length, features = tokens.shape
    heads = bias_table.shape[0]
    attention_hidden = low(normalize(tokens, gain_attn))

    def project(weight_matrix):
        matrix_product = jnp.einsum('awi,ib->awb', attention_hidden, weight_matrix, precision=TOP_PRECISION)
        return reduced_backward(low(matrix_product)).reshape(sequences, length, heads, HEAD_DIM)
    queries = project(w_query)
    key_heads = project(w_key)
    value_heads = project(w_value)
    positions = jnp.arange(length, dtype=jnp.int32)
    offsets = (positions[None, :] - positions[:, None] + length - 1).astype(jnp.int32)
    bias = bias_table[:, bucket_id][:, offsets]
    group = 1
    while group * 2 * length <= 4096 and sequences % (group * 2) == 0:
        group = group * 2
    grouped_shape = (sequences // group, group, length, heads, HEAD_DIM)

    def one_group(items):
        return attention(items[0], items[1], items[2], bias)
    mixed_state = lax.map(jax.checkpoint(one_group), (queries.reshape(grouped_shape), key_heads.reshape(grouped_shape), value_heads.reshape(grouped_shape)))
    mixed_state = mixed_state.reshape(sequences, length, features)
    branch_result = reduced_backward(jnp.einsum('awi,ib->awb', mixed_state, output_weight, precision=TOP_PRECISION))
    after_attn = tokens + branch_result
    mixture_hidden = low(normalize(after_attn, gain_moe))
    router_logits = reduced_backward(jnp.einsum('awi,ib->awb', mixture_hidden, router_weight, precision=TOP_PRECISION))
    gate_probs = softmax_rows(router_logits)
    experts = router_weight.shape[1]
    chosen = (expert_id[:, :, None] == jnp.arange(experts, dtype=jnp.int32)[None, None, :]).astype(jnp.float32)
    picked = lax.optimization_barrier(jnp.sum(gate_probs * chosen, axis=-1, keepdims=True))
    blocks = sequences * N_SEQ
    per_block = length // N_SEQ
    slot_of = jnp.where(slot_id >= 0, expert_id * CAP + slot_id, -1).astype(jnp.int32).reshape(blocks, per_block)
    dispatch = (slot_of[:, :, None] == jnp.arange(experts * CAP, dtype=jnp.int32)[None, None, :]).astype(jnp.float32)
    buffer = jnp.einsum('bts,btd->bsd', dispatch, mixture_hidden.reshape(blocks, per_block, features), precision=TOP_PRECISION)
    buffer = reduced_backward(buffer)
    by_expert = buffer.reshape(blocks, experts, CAP, features).transpose(1, 0, 2, 3)
    by_expert = by_expert.reshape(experts, blocks * CAP, features)
    inner = w_expert_in.reshape(experts, 2, features, -1)
    outer = w_expert_out.reshape(experts, 2, -1, features)

    def one_expert(items):
        received, inner_pair, outer_pair = items
        partials = []
        for half_index in range(2):
            local_rows = reduced_backward(received)
            pre_act = reduced_backward(jnp.dot(local_rows, inner_pair[half_index], precision=TOP_PRECISION, preferred_element_type=jnp.float32))
            activated = low(jax.nn.gelu(pre_act))
            partials.append(low(jnp.dot(activated, outer_pair[half_index], precision=TOP_PRECISION, preferred_element_type=jnp.float32)))
        return reduced_backward(low(partials[0] + partials[1]))
    results = lax.map(jax.checkpoint(one_expert), (by_expert, inner, outer))
    expert_slots = results.reshape(experts, blocks, CAP, features).transpose(1, 0, 2, 3)
    expert_slots = expert_slots.reshape(blocks, experts * CAP, features)
    combined = jnp.einsum('bts,bsd->btd', dispatch, expert_slots, precision=TOP_PRECISION)
    combined = combined.reshape(sequences, length, features)
    return after_attn + picked * combined

def reference(tokens_in, w_query, w_key, w_value, output_weight, gain_attn, gain_moe, router_weight, bias_table, w_expert_in, w_expert_out, expert_id, slot_id, bucket_id, cotangent):
    floats = (tokens_in.astype(jnp.float32), w_query.astype(jnp.float32), w_key.astype(jnp.float32), w_value.astype(jnp.float32), output_weight.astype(jnp.float32), gain_attn.astype(jnp.float32), gain_moe.astype(jnp.float32), router_weight.astype(jnp.float32), bias_table.astype(jnp.float32), w_expert_in.astype(jnp.float32), w_expert_out.astype(jnp.float32))

    def closed(*values):
        return forward(*values, expert_id, slot_id, bucket_id)
    block_out, pull = jax.vjp(closed, *floats)
    grads = pull(cotangent.astype(jnp.float32))
    return (block_out.astype(jnp.bfloat16), grads[0], grads[1], grads[2], grads[3], grads[4], grads[5], grads[6], grads[7], grads[8], grads[9], grads[10])
```

```python
import functools

import jax
import jax.numpy as jnp
from jax import lax
from jax.experimental import pallas as pl
from jax.experimental.pallas import tpu as pltpu
from jax.sharding import PartitionSpec as P

HEAD_DIM = 64
EPS = 1e-06
MESH = pl.DeviceIdType.MESH
VMEM_LIMIT = 56 * 1024 * 1024
BF16 = jnp.bfloat16
F32 = jnp.float32


def round_up(value, step):
    return (value + step - 1) // step * step


def coordinates(bits):
    shard = lax.axis_index("shard")
    return [lax.axis_index("seq")] + [(shard // 2**b) % 2 for b in reversed(range(bits))]


def partner(dim, bits):
    seq, shard = lax.axis_index("seq"), lax.axis_index("shard")
    if dim == 0:
        return (1 - seq, shard)
    step = 2 ** (bits - dim)
    return (seq, shard + (1 - 2 * ((shard // step) % 2)) * step)


def greet(targets):
    barrier = pltpu.get_barrier_semaphore()
    for target in targets:
        pl.semaphore_signal(barrier, inc=1, device_id=target, device_id_type=MESH)
    pl.semaphore_wait(barrier, len(targets))


def gather_orders(bits):
    far = list(range(1, bits - 1))
    near = bits - 1
    return [far + [near, 0, bits], [0, near] + far + [bits]]


def gather_kernel(bits, cuts, pack_ref, tok_ref, table_ref, out_ref, toks_ref, tables_ref, local_sem, send_sem, recv_sem, tok_sem):
    coords = coordinates(bits)
    dims = bits + 1
    greet([partner(d, bits) for d in range(dims)])
    other = partner(0, bits)
    seq = coords[0]
    extras = []
    for n, (src, dst) in enumerate(((tok_ref, toks_ref), (table_ref, tables_ref))):
        copy = pltpu.make_async_remote_copy(
            src, dst.at[seq], tok_sem.at[0, n], tok_sem.at[1, n], device_id=other, device_id_type=MESH
        )
        keep = pltpu.make_async_copy(src, dst.at[seq], tok_sem.at[2, n])
        copy.start()
        keep.start()
        extras += [copy, keep]
    own = pltpu.make_async_copy(pack_ref, out_ref.at[tuple(coords)], local_sem)
    own.start()
    orders = gather_orders(bits)
    done = [[] for _ in cuts]
    flying = [None for _ in cuts]
    sent = []
    for step in range(dims):
        for part, (start, rows) in enumerate(cuts):
            dim = orders[part][step]
            if step == 0:
                src = pack_ref.at[pl.ds(start, rows)]
                dst = out_ref.at[tuple(coords) + (pl.ds(start, rows),)]
            else:
                if step == 1 and part == 0:
                    own.wait()
                flying[part].wait_recv()
                where = tuple(slice(None) if d in done[part] else coords[d] for d in range(dims))
                src = out_ref.at[where + (pl.ds(start, rows),)]
                dst = src
            copy = pltpu.make_async_remote_copy(
                src,
                dst,
                send_sem.at[part, step],
                recv_sem.at[part, step],
                device_id=partner(dim, bits),
                device_id_type=MESH,
            )
            copy.start()
            sent.append(copy)
            flying[part] = copy
            done[part].append(dim)
    for copy in flying:
        copy.wait_recv()
    for copy in sent:
        copy.wait_send()
    for copy in extras:
        copy.wait()


def gather_all(pack, tokens, table, bits):
    rows, columns = pack.shape
    cuts = [(0, 48), (48, rows - 48)] if rows > 64 else [(0, rows)]
    lead = (2,) * (bits + 1)
    any_spec = pl.BlockSpec(memory_space=pl.ANY)
    return pl.pallas_call(
        functools.partial(gather_kernel, bits, cuts),
        out_shape=(
            jax.ShapeDtypeStruct(lead + (rows, columns), BF16),
            jax.ShapeDtypeStruct((2,) + tokens.shape, BF16),
            jax.ShapeDtypeStruct((2,) + table.shape, BF16),
        ),
        in_specs=[any_spec] * 3,
        out_specs=(any_spec,) * 3,
        scratch_shapes=[
            pltpu.SemaphoreType.DMA,
            pltpu.SemaphoreType.DMA((len(cuts), bits + 1)),
            pltpu.SemaphoreType.DMA((len(cuts), bits + 1)),
            pltpu.SemaphoreType.DMA((3, 2)),
        ],
        compiler_params=pltpu.CompilerParams(collective_id=0, has_side_effects=True, vmem_limit_bytes=VMEM_LIMIT),
    )(pack, tokens, table)


def reduce_kernel(bits, parts, *refs):
    ins, table_ref, far_ref = refs[:parts], refs[parts], refs[parts + 1]
    outs, table_out, far_out = refs[parts + 2 : 2 * parts + 2], refs[2 * parts + 2], refs[2 * parts + 3]
    rest = list(refs[2 * parts + 4 :])
    dims = bits + 1
    landed = [rest[p * dims : (p + 1) * dims] for p in range(parts)]
    rest = rest[parts * dims :]
    sums = [rest[p * bits : (p + 1) * bits] for p in range(parts)]
    rest = rest[parts * bits :]
    table_landed, table_sums, send_sem, recv_sem, table_sem, far_sem = rest
    coords = coordinates(bits)
    greet([partner(d, bits) for d in range(dims)])
    far_copy = pltpu.make_async_remote_copy(
        far_ref, far_out, far_sem.at[0], far_sem.at[1], device_id=partner(0, bits), device_id_type=MESH
    )
    far_copy.start()
    orders = [list(reversed(order)) for order in gather_orders(bits)]
    held = list(ins)
    left = [list(range(dims)) for _ in range(parts)]
    sent = [far_copy]
    table_now = table_ref
    for step in range(dims):
        flying = []
        for part in range(parts):
            dim = orders[part][step]
            spot = left[part].index(dim)
            whole = (slice(None),) * spot
            copy = pltpu.make_async_remote_copy(
                held[part].at[whole + (1 - coords[dim],)],
                landed[part][step],
                send_sem.at[part, step],
                recv_sem.at[part, step],
                device_id=partner(dim, bits),
                device_id_type=MESH,
            )
            copy.start()
            sent.append(copy)
            flying.append((copy, whole, dim))
        small = pltpu.make_async_remote_copy(
            table_now,
            table_landed.at[step],
            table_sem.at[0, step],
            table_sem.at[1, step],
            device_id=partner(step, bits),
            device_id_type=MESH,
        )
        small.start()
        sent.append(small)
        for part, (copy, whole, dim) in enumerate(flying):
            copy.wait_recv()
            total = held[part][whole + (coords[dim],)].astype(F32) + landed[part][step][...].astype(F32)
            left[part].remove(dim)
            if step == dims - 1:
                outs[part][...] = total
            else:
                sums[part][step][...] = total.astype(BF16)
                held[part] = sums[part][step]
        small.wait_recv()
        total = table_now[...] + table_landed[step]
        if step == dims - 1:
            table_out[...] = total
        else:
            table_sums[step] = total
            table_now = table_sums.at[step]
    far_copy.wait_recv()
    for copy in sent:
        copy.wait_send()


def reduce_all(parts, table, far, bits):
    dims = bits + 1
    vmem = pl.BlockSpec(memory_space=pltpu.VMEM)
    count = len(parts)
    scratch = []
    for part in parts:
        scratch += [pltpu.VMEM((2,) * (dims - 1 - s) + part.shape[-2:], BF16) for s in range(dims)]
    for part in parts:
        scratch += [pltpu.VMEM((2,) * (dims - 1 - s) + part.shape[-2:], BF16) for s in range(dims - 1)]
    scratch += [
        pltpu.VMEM((dims,) + table.shape, F32),
        pltpu.VMEM((dims,) + table.shape, F32),
        pltpu.SemaphoreType.DMA((count, dims)),
        pltpu.SemaphoreType.DMA((count, dims)),
        pltpu.SemaphoreType.DMA((2, dims)),
        pltpu.SemaphoreType.DMA((2,)),
    ]
    return pl.pallas_call(
        functools.partial(reduce_kernel, bits, count),
        out_shape=tuple(jax.ShapeDtypeStruct(part.shape[-2:], F32) for part in parts)
        + (jax.ShapeDtypeStruct(table.shape, F32), jax.ShapeDtypeStruct(far.shape, BF16)),
        in_specs=[vmem] * (count + 2),
        out_specs=(vmem,) * (count + 2),
        scratch_shapes=scratch,
        compiler_params=pltpu.CompilerParams(collective_id=1, has_side_effects=True, vmem_limit_bytes=VMEM_LIMIT),
    )(*parts, table, far)


def contract(a, b, on_a, on_b):
    return lax.dot_general(a, b, (((on_a,), (on_b,)), ((), ())), preferred_element_type=F32)


GELU_SCALE = 0.7978845608028654


def expert_kernel(
    chips, buf_ref, grad_ref, w_in_ref, w_out_ref, slots_ref, gslots_ref, wgrad_ref,
    rows_x, rows_g, act_ref, gpre_ref, part_ref, sib_ref, ret_ref,
    in_sem, fwd_sem, sib_sem, out_sem,
):
    seq, shard = lax.axis_index("seq"), lax.axis_index("shard")
    chip, core = shard // 2, shard % 2
    sibling = (seq, shard + 1 - 2 * core)
    capacity, width = buf_ref.shape[1:]
    hidden = w_in_ref.shape[1]

    def device_of(other):
        return (seq, 2 * other + core)

    greet([device_of((chip + j) % chips) for j in range(1, chips)] + [sibling])
    pairs = ((buf_ref, rows_x), (grad_ref, rows_g))
    sent = []
    copies = {}
    for j in range(1, chips):
        to = (chip + j) % chips
        for n, (src, dst) in enumerate(pairs):
            copy = pltpu.make_async_remote_copy(
                src.at[to], dst.at[chip, core], in_sem.at[0, n, j], in_sem.at[1, n, j],
                device_id=device_of(to), device_id_type=MESH,
            )
            copy.start()
            copies[n, j] = copy
            sent.append(copy)
    for n, (src, dst) in enumerate(pairs):
        dst[chip, core] = src[chip]
    forwards = []
    for j in range(chips):
        source = (chip + chips - j) % chips
        for n, (src, dst) in enumerate(pairs):
            if j:
                copies[n, j].wait_recv()
            copy = pltpu.make_async_remote_copy(
                dst.at[source, core], dst.at[source, core], fwd_sem.at[0, n, j], fwd_sem.at[1, n, j],
                device_id=sibling, device_id_type=MESH,
            )
            copy.start()
            forwards.append(copy)
            sent.append(copy)
    for copy in forwards:
        copy.wait_recv()

    group = max(1, 256 // (2 * capacity))
    block = group * 2 * capacity
    piece = 512

    @pl.loop(0, chips // group)
    def _(t):
        x = rows_x[pl.ds(t * group, group)].reshape(block, width)
        g = rows_g[pl.ds(t * group, group)].reshape(block, width)
        out_sum = jnp.zeros((block, width), F32)
        half_sum = jnp.zeros((block, width), F32)
        where = pl.ds(pl.multiple_of(t * block, block), block)
        for h in range(hidden // piece):
            cols = pl.ds(h * piece, piece)
            pre = jnp.dot(x, w_in_ref[:, cols], preferred_element_type=F32)
            gact = contract(g, w_out_ref[cols, :], 1, 1)
            square = pre * pre
            t_val = jnp.tanh(GELU_SCALE * (pre + 0.044715 * square * pre))
            act = (0.5 * pre * (1.0 + t_val)).astype(BF16)
            slope = 0.5 * (1.0 + t_val) + 0.5 * pre * (1.0 - t_val * t_val) * (
                GELU_SCALE * (1.0 + 0.134145 * square)
            )
            gpre = (gact * slope).astype(BF16)
            act_ref[where, cols] = act
            gpre_ref[where, cols] = gpre
            out_sum += jnp.dot(act, w_out_ref[cols, :], preferred_element_type=F32)
            half_sum += contract(gpre, w_in_ref[:, cols], 1, 1)
        out_b = out_sum.astype(BF16).reshape(group, 2, capacity, width)
        half_b = half_sum.astype(BF16).reshape(group, 2, capacity, width)
        for u in range(2):
            part_ref[0, u, pl.ds(t * group, group)] = out_b[:, u]
            part_ref[1, u, pl.ds(t * group, group)] = half_b[:, u]

    swaps = []
    for n in range(2):
        copy = pltpu.make_async_remote_copy(
            part_ref.at[n, 1 - core], sib_ref.at[n], sib_sem.at[0, n], sib_sem.at[1, n],
            device_id=sibling, device_id_type=MESH,
        )
        copy.start()
        swaps.append(copy)
        sent.append(copy)
    returns = []
    outs = (slots_ref, gslots_ref)
    for n in range(2):
        swaps[n].wait_recv()
        ret_ref[n] = (part_ref[n, core].astype(F32) + sib_ref[n].astype(F32)).astype(BF16)
        for j in range(1, chips):
            to = (chip + j) % chips
            copy = pltpu.make_async_remote_copy(
                ret_ref.at[n, to], outs[n].at[chip], out_sem.at[0, n, j], out_sem.at[1, n, j],
                device_id=device_of(to), device_id_type=MESH,
            )
            copy.start()
            returns.append(copy)
            sent.append(copy)
        outs[n][chip] = ret_ref[n, chip]
    all_x = rows_x[...].reshape(-1, width)
    all_g = rows_g[...].reshape(-1, width)
    side = hidden // 2
    for h in range(2):
        cols = pl.ds(h * side, side)
        wgrad_ref[h, 0] = contract(all_x, gpre_ref[:, cols], 0, 0).astype(BF16)
        wgrad_ref[h, 1] = contract(act_ref[:, cols], all_g, 0, 0).astype(BF16)
    for copy in returns:
        copy.wait_recv()
    for copy in sent:
        copy.wait_send()


def run_experts(buffer, grad_slots, w_in, w_out):
    chips, capacity, width = buffer.shape
    hidden = w_in.shape[1]
    rows = chips * 2 * capacity
    vmem = pl.BlockSpec(memory_space=pltpu.VMEM)
    return pl.pallas_call(
        functools.partial(expert_kernel, chips),
        out_shape=(
            jax.ShapeDtypeStruct(buffer.shape, BF16),
            jax.ShapeDtypeStruct(buffer.shape, BF16),
            jax.ShapeDtypeStruct((2, 2, width, hidden // 2), BF16),
        ),
        in_specs=[vmem] * 4,
        out_specs=(vmem,) * 3,
        scratch_shapes=[
            pltpu.VMEM((chips, 2, capacity, width), BF16),
            pltpu.VMEM((chips, 2, capacity, width), BF16),
            pltpu.VMEM((rows, hidden), BF16),
            pltpu.VMEM((rows, hidden), BF16),
            pltpu.VMEM((2, 2, chips, capacity, width), BF16),
            pltpu.VMEM((2, chips, capacity, width), BF16),
            pltpu.VMEM((2, chips, capacity, width), BF16),
            pltpu.SemaphoreType.DMA((2, 2, chips)),
            pltpu.SemaphoreType.DMA((2, 2, chips)),
            pltpu.SemaphoreType.DMA((2, 2)),
            pltpu.SemaphoreType.DMA((2, 2, chips)),
        ],
        compiler_params=pltpu.CompilerParams(collective_id=2, has_side_effects=True, vmem_limit_bytes=VMEM_LIMIT),
    )(buffer, grad_slots, w_in, w_out)


def rms_parts(values):
    inverse = lax.rsqrt(jnp.mean(values * values, axis=-1, keepdims=True) + EPS)
    return (values * inverse, inverse)


def rms_back(grad_normed, normed, inverse):
    return inverse * (grad_normed - normed * jnp.mean(grad_normed * normed, axis=-1, keepdims=True))


def spread_offsets(per_offset, block_rows, columns):
    heads_here = per_offset.shape[0]
    period = block_rows + columns
    padded = jnp.pad(per_offset, ((0, 0), (0, 1)))
    tiled = jnp.tile(padded, (1, block_rows))[:, : block_rows * (period - 1)]
    return tiled.reshape(heads_here, block_rows, period - 1)[:, :, block_rows - 1 :]


def offset_sums(grid):
    heads_here, block_rows, columns = grid.shape
    period = block_rows + columns
    widened = jnp.pad(grid, ((0, 0), (0, 0), (block_rows - 1, 0)))
    flat_grid = widened.reshape(heads_here, block_rows * (period - 1))
    flat_grid = jnp.pad(flat_grid, ((0, 0), (0, block_rows)))
    return jnp.sum(flat_grid.reshape(heads_here, block_rows, period), axis=1)[:, : period - 1]


def heads_of(matrix):
    return matrix.reshape(matrix.shape[0], -1, HEAD_DIM)


def local(
    devices_along_shard, tokens_in, w_query, w_key, w_value, output_weight, gain_attn, gain_moe, router_weight,
    bias_table, w_expert_in, w_expert_out, expert_id, slot_id, bucket_id, cotangent,
):
    bits = devices_along_shard.bit_length() - 1
    devices = 2 * devices_along_shard
    seq = lax.axis_index("seq")
    rows, width = w_query.shape
    experts = router_weight.shape[1]
    tokens_here = tokens_in.shape[1]
    length = 2 * tokens_here
    capacity = 2 * max(1, 5 * tokens_here // (8 * experts))
    slots = round_up(capacity, 16)
    pack_rows = round_up(4 * rows + 1, 16)
    heads_side, buckets = bias_table.shape

    extra = jnp.concatenate([router_weight.reshape(-1), gain_attn, gain_moe])
    extra = jnp.pad(extra, (0, width - extra.shape[0]))[None]
    pack = jnp.concatenate([w_query, w_key, w_value, output_weight, extra], axis=0)
    pack = jnp.pad(pack, ((0, pack_rows - pack.shape[0]), (0, 0)))
    table_tile = jnp.pad(bias_table, ((0, 16 - heads_side), (0, 128 - buckets)))
    gathered, both_tokens, both_tables = gather_all(pack, tokens_in[0], table_tile, bits)
    gathered = gathered.reshape(devices, pack_rows, width)
    full_query, full_key, full_value, full_output = (
        gathered[:, n * rows : (n + 1) * rows].reshape(width, width) for n in range(4)
    )
    extra = gathered[:, 4 * rows]
    cut = rows * experts
    full_router = extra[:, :cut].reshape(width, experts)
    full_gain_attn = extra[:, cut : cut + rows].reshape(width).astype(F32)
    full_gain_moe = extra[:, cut + rows : cut + 2 * rows].reshape(width).astype(F32)
    full_table = both_tables[:, :heads_side, :buckets].reshape(2 * heads_side, buckets)

    def mine(array):
        return lax.dynamic_slice_in_dim(array, seq * tokens_here, tokens_here, 0)

    inputs = tokens_in[0].astype(F32)
    normed_all, _ = rms_parts(both_tokens.reshape(length, width).astype(F32))
    normed_attn, inverse_attn = rms_parts(inputs)
    hidden_all = (normed_all * full_gain_attn).astype(BF16)
    hidden_own = (normed_attn * full_gain_attn).astype(BF16)
    queries = heads_of(jnp.dot(hidden_own, full_query, preferred_element_type=F32).astype(BF16))
    keys = heads_of(jnp.dot(hidden_all, full_key, preferred_element_type=F32).astype(BF16))
    values = heads_of(jnp.dot(hidden_all, full_value, preferred_element_type=F32).astype(BF16))

    bucket_onehot = (jnp.arange(buckets, dtype=jnp.int32)[:, None] == bucket_id[None, :]).astype(BF16)
    onehot_here = lax.dynamic_slice_in_dim(
        bucket_onehot, tokens_here * (1 - seq), tokens_here + length - 1, 1
    )
    per_offset = jnp.dot(full_table, onehot_here, preferred_element_type=F32)
    scores = jnp.einsum("qhd,khd->hqk", queries, keys, preferred_element_type=F32)
    scores = scores + spread_offsets(per_offset, tokens_here, length)
    weights = jnp.exp(scores - jnp.max(scores, axis=-1, keepdims=True))
    probs = weights / jnp.sum(weights, axis=-1, keepdims=True)
    probs_low = probs.astype(BF16)
    mixed = jnp.einsum("hqk,khd->qhd", probs_low, values, preferred_element_type=F32)
    mixed = mixed.reshape(tokens_here, width).astype(BF16)

    after_attn = inputs + jnp.dot(mixed, full_output, preferred_element_type=F32)
    normed_moe, inverse_moe = rms_parts(after_attn)
    hidden_moe = (normed_moe * full_gain_moe).astype(BF16)
    router_logits = jnp.dot(hidden_moe, full_router, preferred_element_type=F32)
    gate_weights = jnp.exp(router_logits - jnp.max(router_logits, axis=-1, keepdims=True))
    gate_probs = gate_weights / jnp.sum(gate_weights, axis=-1, keepdims=True)
    chosen = (expert_id[0][:, None] == jnp.arange(experts, dtype=jnp.int32)[None, :]).astype(F32)
    picked = jnp.sum(gate_probs * chosen, axis=-1, keepdims=True)
    slot_of = jnp.where(slot_id[0] >= 0, expert_id[0] * slots + slot_id[0], -1)
    dispatch = (slot_of[:, None] == jnp.arange(experts * slots, dtype=jnp.int32)[None, :]).astype(BF16)
    grad_out = cotangent[0].astype(F32)
    scaled = (picked * grad_out).astype(BF16)
    buffer = contract(dispatch, hidden_moe, 0, 0).astype(BF16)
    grad_slots = contract(dispatch, scaled, 0, 0).astype(BF16)
    expert_slots, grad_buffer, expert_grads = run_experts(
        buffer.reshape(experts, slots, width),
        grad_slots.reshape(experts, slots, width),
        w_expert_in[0],
        w_expert_out[0],
    )
    leaving = lax.dynamic_index_in_dim(expert_grads, 1 - seq, 0, keepdims=False)
    arriving = lax.ppermute(leaving, "seq", [(0, 1), (1, 0)])

    combined = jnp.dot(dispatch, expert_slots.reshape(-1, width), preferred_element_type=F32)
    block_out = after_attn + picked * combined
    grad_picked = jnp.sum(grad_out * combined, axis=-1, keepdims=True)
    grad_gates = chosen * grad_picked
    grad_logits = gate_probs * (grad_gates - jnp.sum(gate_probs * grad_gates, axis=-1, keepdims=True))
    grad_logits = grad_logits.astype(BF16)
    grad_router = contract(hidden_moe, grad_logits, 0, 0)
    grad_hidden_moe = contract(grad_logits, full_router, 1, 1)
    grad_hidden_moe = grad_hidden_moe + jnp.dot(
        dispatch, grad_buffer.reshape(-1, width), preferred_element_type=F32
    )
    grad_gain_moe = jnp.sum(grad_hidden_moe * normed_moe, axis=0)
    grad_mid = grad_out + rms_back(grad_hidden_moe * full_gain_moe, normed_moe, inverse_moe)
    grad_branch = grad_mid.astype(BF16)
    grad_output = contract(mixed, grad_branch, 0, 0)
    grad_mixed = heads_of(contract(grad_branch, full_output, 1, 1).astype(BF16))

    grad_probs = jnp.einsum("qhd,khd->hqk", grad_mixed, values, preferred_element_type=F32)
    centre = jnp.sum(probs * grad_probs, axis=-1, keepdims=True)
    grad_scores = (probs * (grad_probs - centre)).astype(BF16)
    grad_q = jnp.einsum("hqk,khd->qhd", grad_scores, keys, preferred_element_type=F32)
    grad_k = jnp.einsum("hqk,qhd->khd", grad_scores, queries, preferred_element_type=F32)
    grad_v = jnp.einsum("hqk,qhd->khd", probs_low, grad_mixed, preferred_element_type=F32)
    grad_q = grad_q.reshape(tokens_here, width).astype(BF16)
    grad_k = grad_k.reshape(length, width).astype(BF16)
    grad_v = grad_v.reshape(length, width).astype(BF16)
    grad_offset = offset_sums(grad_scores.astype(F32))
    grad_table = jnp.einsum(
        "ho,bo->hb", grad_offset, onehot_here.astype(F32), precision=lax.Precision.HIGHEST
    )
    grad_table = jnp.pad(grad_table, ((0, 16 - 2 * heads_side), (0, 128 - buckets)))

    back_query = contract(grad_q, full_query, 1, 1)
    back_all = contract(grad_k, full_key, 1, 1) + contract(grad_v, full_value, 1, 1)
    grad_gain_attn = jnp.sum(back_query * normed_attn, axis=0) + jnp.sum(back_all * normed_all, axis=0)
    far = lax.dynamic_slice_in_dim(back_all, (1 - seq) * tokens_here, tokens_here, 0).astype(BF16)

    def by_device(matrix):
        return matrix.reshape(devices, rows, width).astype(BF16)

    extra = jnp.concatenate(
        [
            grad_router.reshape(devices, rows * experts),
            grad_gain_attn.reshape(devices, rows),
            grad_gain_moe.reshape(devices, rows),
        ],
        axis=1,
    )
    extra = jnp.pad(extra, ((0, 0), (0, width - extra.shape[1])))[:, None].astype(BF16)
    pieces = [
        by_device(contract(hidden_own, grad_q, 0, 0)),
        by_device(contract(hidden_all, grad_k, 0, 0)),
        by_device(contract(hidden_all, grad_v, 0, 0)),
        by_device(grad_output),
        extra,
    ]
    lead = (2,) * (bits + 1)

    def joined(some):
        part = jnp.concatenate(some, axis=1)
        part = jnp.pad(part, ((0, 0), (0, round_up(part.shape[1], 16) - part.shape[1]), (0, 0)))
        return part.reshape(lead + part.shape[1:])

    parts = [joined(pieces[:2]), joined(pieces[2:])] if rows % 8 == 0 else [joined(pieces)]
    *sums, table_sum, far_sum = reduce_all(parts, grad_table, far, bits)
    total = jnp.concatenate([sums[0][: 2 * rows], *sums[1:]], axis=0) if len(sums) > 1 else sums[0]
    share = total[4 * rows]

    grad_hidden_attn = back_query + mine(back_all) + far_sum.astype(F32)
    grad_tokens = grad_mid + rms_back(grad_hidden_attn * full_gain_attn, normed_attn, inverse_attn)
    kept = lax.dynamic_index_in_dim(expert_grads, seq, 0, keepdims=False)
    expert_sum = kept.astype(F32) + arriving.astype(F32)
    return (
        block_out.astype(BF16)[None],
        grad_tokens[None],
        total[:rows],
        total[rows : 2 * rows],
        total[2 * rows : 3 * rows],
        total[3 * rows : 4 * rows],
        share[cut : cut + rows],
        share[cut + rows : cut + 2 * rows],
        share[:cut].reshape(rows, experts),
        lax.dynamic_slice_in_dim(table_sum[:, :buckets], seq * heads_side, heads_side, 0),
        expert_sum[0][None],
        expert_sum[1][None],
    )


def solution(mesh):
    return jax.shard_map(
        functools.partial(local, mesh.shape["shard"]),
        mesh=mesh,
        in_specs=(
            P("shard", "seq", None),
            P(("seq", "shard"), None),
            P(("seq", "shard"), None),
            P(("seq", "shard"), None),
            P(("seq", "shard"), None),
            P(("seq", "shard")),
            P(("seq", "shard")),
            P(("seq", "shard"), None),
            P("seq", None),
            P("shard", None, None),
            P("shard", None, None),
            P("shard", "seq"),
            P("shard", "seq"),
            P(),
            P("shard", "seq", None),
        ),
        out_specs=(
            P("shard", "seq", None),
            P("shard", "seq", None),
            P(("seq", "shard"), None),
            P(("seq", "shard"), None),
            P(("seq", "shard"), None),
            P(("seq", "shard"), None),
            P(("seq", "shard")),
            P(("seq", "shard")),
            P(("seq", "shard"), None),
            P("seq", None),
            P("shard", None, "seq"),
            P("shard", "seq", None),
        ),
        check_vma=False,
    )
```

```python
import functools

import jax
import jax.numpy as jnp
from jax import lax
from jax.experimental import pallas as pl
from jax.experimental.pallas import tpu as pltpu
from jax.sharding import PartitionSpec as P

HEAD_DIM = 64
EPS = 1e-06
MESH = pl.DeviceIdType.MESH
VMEM_LIMIT = 56 * 1024 * 1024
BF16 = jnp.bfloat16
F32 = jnp.float32


def round_up(value, step):
    return (value + step - 1) // step * step


def coordinates(bits):
    shard = lax.axis_index("shard")
    return [lax.axis_index("seq")] + [(shard // 2**b) % 2 for b in reversed(range(bits))]


def partner(dim, bits):
    seq, shard = lax.axis_index("seq"), lax.axis_index("shard")
    if dim == 0:
        return (1 - seq, shard)
    step = 2 ** (bits - dim)
    return (seq, shard + (1 - 2 * ((shard // step) % 2)) * step)


def greet(targets):
    barrier = pltpu.get_barrier_semaphore()
    for target in targets:
        pl.semaphore_signal(barrier, inc=1, device_id=target, device_id_type=MESH)
    pl.semaphore_wait(barrier, len(targets))


def gather_plan(rows, bits):
    far, near = list(range(1, bits - 1)), bits - 1
    orders = [far + [near, 0, bits], far + [0, near, bits]]
    size = 32 if rows > 64 else rows
    starts = range(0, rows, size)
    return [(start, min(size, rows - start), orders[n % 2]) for n, start in enumerate(starts)]


def gather_kernel(bits, plan, pack_ref, tok_ref, table_ref, out_ref, toks_ref, tables_ref, local_sem, send_sem, recv_sem, tok_sem):
    coords = coordinates(bits)
    dims = bits + 1
    greet([partner(d, bits) for d in range(dims)])
    other = partner(0, bits)
    seq = coords[0]
    extras = []
    for n, (src, dst) in enumerate(((tok_ref, toks_ref), (table_ref, tables_ref))):
        copy = pltpu.make_async_remote_copy(
            src, dst.at[seq], tok_sem.at[0, n], tok_sem.at[1, n], device_id=other, device_id_type=MESH
        )
        keep = pltpu.make_async_copy(src, dst.at[seq], tok_sem.at[2, n])
        copy.start()
        keep.start()
        extras += [copy, keep]
    own = pltpu.make_async_copy(pack_ref, out_ref.at[tuple(coords)], local_sem)
    own.start()
    done = [[] for _ in plan]
    flying = [None for _ in plan]
    sent = []
    for step in range(dims):
        for part, (start, rows, order) in enumerate(plan):
            dim = order[step]
            if step == 0:
                src = pack_ref.at[pl.ds(start, rows)]
                dst = out_ref.at[tuple(coords) + (pl.ds(start, rows),)]
            else:
                if step == 1 and part == 0:
                    own.wait()
                flying[part].wait_recv()
                where = tuple(slice(None) if d in done[part] else coords[d] for d in range(dims))
                src = out_ref.at[where + (pl.ds(start, rows),)]
                dst = src
            copy = pltpu.make_async_remote_copy(
                src,
                dst,
                send_sem.at[part, step],
                recv_sem.at[part, step],
                device_id=partner(dim, bits),
                device_id_type=MESH,
            )
            copy.start()
            sent.append(copy)
            flying[part] = copy
            done[part].append(dim)
    for copy in flying:
        copy.wait_recv()
    for copy in sent:
        copy.wait_send()
    for copy in extras:
        copy.wait()


def gather_all(pack, tokens, table, bits):
    rows, columns = pack.shape
    plan = gather_plan(rows, bits)
    lead = (2,) * (bits + 1)
    any_spec = pl.BlockSpec(memory_space=pl.ANY)
    return pl.pallas_call(
        functools.partial(gather_kernel, bits, plan),
        out_shape=(
            jax.ShapeDtypeStruct(lead + (rows, columns), BF16),
            jax.ShapeDtypeStruct((2,) + tokens.shape, BF16),
            jax.ShapeDtypeStruct((2,) + table.shape, BF16),
        ),
        in_specs=[any_spec] * 3,
        out_specs=(any_spec,) * 3,
        scratch_shapes=[
            pltpu.SemaphoreType.DMA,
            pltpu.SemaphoreType.DMA((len(plan), bits + 1)),
            pltpu.SemaphoreType.DMA((len(plan), bits + 1)),
            pltpu.SemaphoreType.DMA((3, 2)),
        ],
        compiler_params=pltpu.CompilerParams(collective_id=0, has_side_effects=True, vmem_limit_bytes=VMEM_LIMIT),
    )(pack, tokens, table)


def reduce_kernel(bits, plan, in_ref, table_ref, far_ref, out_ref, table_out, far_out, *rest):
    parts, dims = len(plan), bits + 1
    rest = list(rest)
    landed = [rest[p * dims : (p + 1) * dims] for p in range(parts)]
    rest = rest[parts * dims :]
    sums = [rest[p * bits : (p + 1) * bits] for p in range(parts)]
    rest = rest[parts * bits :]
    table_landed, table_sums, send_sem, recv_sem, table_sem, far_sem = rest
    coords = coordinates(bits)
    greet([partner(d, bits) for d in range(dims)])
    far_copy = pltpu.make_async_remote_copy(
        far_ref, far_out, far_sem.at[0], far_sem.at[1], device_id=partner(0, bits), device_id_type=MESH
    )
    far_copy.start()
    orders = [list(reversed(order)) for _, _, order in plan]
    held = [in_ref.at[(slice(None),) * dims + (pl.ds(start, rows),)] for start, rows, _ in plan]
    left = [list(range(dims)) for _ in range(parts)]
    sent = [far_copy]
    table_now = table_ref
    for step in range(dims):
        flying = []
        for part in range(parts):
            dim = orders[part][step]
            spot = left[part].index(dim)
            whole = (slice(None),) * spot
            copy = pltpu.make_async_remote_copy(
                held[part].at[whole + (1 - coords[dim],)],
                landed[part][step],
                send_sem.at[part, step],
                recv_sem.at[part, step],
                device_id=partner(dim, bits),
                device_id_type=MESH,
            )
            copy.start()
            sent.append(copy)
            flying.append((copy, whole, dim))
        small = pltpu.make_async_remote_copy(
            table_now,
            table_landed.at[step],
            table_sem.at[0, step],
            table_sem.at[1, step],
            device_id=partner(step, bits),
            device_id_type=MESH,
        )
        small.start()
        sent.append(small)
        for part, (copy, whole, dim) in enumerate(flying):
            copy.wait_recv()
            total = held[part][whole + (coords[dim],)].astype(F32) + landed[part][step][...].astype(F32)
            left[part].remove(dim)
            if step == dims - 1:
                out_ref[pl.ds(plan[part][0], plan[part][1])] = total
            else:
                sums[part][step][...] = total.astype(BF16)
                held[part] = sums[part][step]
        small.wait_recv()
        total = table_now[...] + table_landed[step]
        if step == dims - 1:
            table_out[...] = total
        else:
            table_sums[step] = total
            table_now = table_sums.at[step]
    far_copy.wait_recv()
    for copy in sent:
        copy.wait_send()


def reduce_all(blocks, table, far, bits):
    dims = bits + 1
    rows, width = blocks.shape[-2:]
    plan = gather_plan(rows, bits)
    vmem = pl.BlockSpec(memory_space=pltpu.VMEM)
    count = len(plan)
    scratch = []
    for _, part_rows, _ in plan:
        scratch += [pltpu.VMEM((2,) * (dims - 1 - s) + (part_rows, width), BF16) for s in range(dims)]
    for _, part_rows, _ in plan:
        scratch += [pltpu.VMEM((2,) * (dims - 1 - s) + (part_rows, width), BF16) for s in range(dims - 1)]
    scratch += [
        pltpu.VMEM((dims,) + table.shape, F32),
        pltpu.VMEM((dims,) + table.shape, F32),
        pltpu.SemaphoreType.DMA((count, dims)),
        pltpu.SemaphoreType.DMA((count, dims)),
        pltpu.SemaphoreType.DMA((2, dims)),
        pltpu.SemaphoreType.DMA((2,)),
    ]
    return pl.pallas_call(
        functools.partial(reduce_kernel, bits, plan),
        out_shape=(
            jax.ShapeDtypeStruct((rows, width), F32),
            jax.ShapeDtypeStruct(table.shape, F32),
            jax.ShapeDtypeStruct(far.shape, BF16),
        ),
        in_specs=[vmem] * 3,
        out_specs=(vmem,) * 3,
        scratch_shapes=scratch,
        compiler_params=pltpu.CompilerParams(collective_id=1, has_side_effects=True, vmem_limit_bytes=VMEM_LIMIT),
    )(blocks, table, far)


def contract(a, b, on_a, on_b):
    return lax.dot_general(a, b, (((on_a,), (on_b,)), ((), ())), preferred_element_type=F32)


GELU_SCALE = 0.7978845608028654


def expert_kernel(
    chips, both_ref, w_in_ref, w_out_ref, back_ref, keep_ref, leave_ref,
    rows_ref, x_ref, g_ref, act_ref, gpre_ref, part_ref, sib_ref, ret_ref,
    in_sem, fwd_sem, sib_sem, out_sem,
):
    seq, shard = lax.axis_index("seq"), lax.axis_index("shard")
    chip, core = shard // 2, shard % 2
    sibling = (seq, shard + 1 - 2 * core)
    slots, width = both_ref.shape[1] // 2, both_ref.shape[2]
    hidden = w_in_ref.shape[1]

    def device_of(other):
        return (seq, 2 * other + core)

    greet([device_of((chip + j) % chips) for j in range(1, chips)] + [sibling])
    sent = []
    copies = {}
    for j in range(1, chips):
        to = (chip + j) % chips
        copy = pltpu.make_async_remote_copy(
            both_ref.at[to], rows_ref.at[chip, core], in_sem.at[0, j], in_sem.at[1, j],
            device_id=device_of(to), device_id_type=MESH,
        )
        copy.start()
        copies[j] = copy
        sent.append(copy)
    rows_ref[chip, core] = both_ref[chip]
    forwards = []
    for j in range(chips):
        source = (chip + chips - j) % chips
        if j:
            copies[j].wait_recv()
        copy = pltpu.make_async_remote_copy(
            rows_ref.at[source, core], rows_ref.at[source, core], fwd_sem.at[0, j], fwd_sem.at[1, j],
            device_id=sibling, device_id_type=MESH,
        )
        copy.start()
        forwards.append(copy)
        sent.append(copy)
    for copy in forwards:
        copy.wait_recv()

    group = chips
    while group * 2 * slots > 512:
        group //= 2
    block = group * 2 * slots
    piece = 512

    @pl.loop(0, chips // group)
    def _(t):
        rows = rows_ref[pl.ds(t * group, group)].astype(F32)
        x = rows[:, :, :slots].reshape(block, width).astype(BF16)
        g = rows[:, :, slots:].reshape(block, width).astype(BF16)
        out_sum = jnp.zeros((block, width), F32)
        half_sum = jnp.zeros((block, width), F32)
        where = pl.ds(pl.multiple_of(t * block, block), block)
        x_ref[where] = x
        g_ref[where] = g
        for h in range(hidden // piece):
            cols = pl.ds(h * piece, piece)
            pre = jnp.dot(x, w_in_ref[:, cols], preferred_element_type=F32)
            gact = contract(g, w_out_ref[cols, :], 1, 1)
            square = pre * pre
            t_val = jnp.tanh(GELU_SCALE * (pre + 0.044715 * square * pre))
            act = (0.5 * pre * (1.0 + t_val)).astype(BF16)
            slope = 0.5 * (1.0 + t_val) + 0.5 * pre * (1.0 - t_val * t_val) * (
                GELU_SCALE * (1.0 + 0.134145 * square)
            )
            gpre = (gact * slope).astype(BF16)
            act_ref[where, cols] = act
            gpre_ref[where, cols] = gpre
            out_sum += jnp.dot(act, w_out_ref[cols, :], preferred_element_type=F32)
            half_sum += contract(gpre, w_in_ref[:, cols], 1, 1)
        out_sum = out_sum.reshape(group, 2, slots, width)
        half_sum = half_sum.reshape(group, 2, slots, width)
        both = jnp.concatenate([out_sum, half_sum], axis=2).astype(BF16)
        for u in range(2):
            part_ref[u, pl.ds(t * group, group)] = both[:, u]

    swap = pltpu.make_async_remote_copy(
        part_ref.at[1 - core], sib_ref, sib_sem.at[0], sib_sem.at[1], device_id=sibling, device_id_type=MESH
    )
    swap.start()
    sent.append(swap)
    side = hidden // 2
    away = pl.ds(pl.multiple_of((1 - seq) * side, side), side)
    home = pl.ds(pl.multiple_of(seq * side, side), side)
    returns = []
    swap.wait_recv()
    ret_ref[...] = (part_ref[core].astype(F32) + sib_ref[...].astype(F32)).astype(BF16)
    for j in range(1, chips):
        to = (chip + j) % chips
        copy = pltpu.make_async_remote_copy(
            ret_ref.at[to], back_ref.at[chip], out_sem.at[0, j], out_sem.at[1, j],
            device_id=device_of(to), device_id_type=MESH,
        )
        copy.start()
        returns.append(copy)
        sent.append(copy)
    back_ref[chip] = ret_ref[chip]
    for target, cols in ((leave_ref, away), (keep_ref, home)):
        target[0] = contract(x_ref[...], gpre_ref[:, cols], 0, 0).astype(BF16)
        target[1] = contract(act_ref[:, cols], g_ref[...], 0, 0).astype(BF16)
    for copy in returns:
        copy.wait_recv()
    for copy in sent:
        copy.wait_send()


def run_experts(both, w_in, w_out):
    chips, doubled, width = both.shape
    hidden = w_in.shape[1]
    rows = chips * doubled
    vmem = pl.BlockSpec(memory_space=pltpu.VMEM)
    half = jax.ShapeDtypeStruct((2, width, hidden // 2), BF16)
    return pl.pallas_call(
        functools.partial(expert_kernel, chips),
        out_shape=(jax.ShapeDtypeStruct(both.shape, BF16), half, half),
        in_specs=[vmem] * 3,
        out_specs=(vmem,) * 3,
        scratch_shapes=[
            pltpu.VMEM((chips, 2, doubled, width), BF16),
            pltpu.VMEM((rows, width), BF16),
            pltpu.VMEM((rows, width), BF16),
            pltpu.VMEM((rows, hidden), BF16),
            pltpu.VMEM((rows, hidden), BF16),
            pltpu.VMEM((2, chips, doubled, width), BF16),
            pltpu.VMEM((chips, doubled, width), BF16),
            pltpu.VMEM((chips, doubled, width), BF16),
            pltpu.SemaphoreType.DMA((2, chips)),
            pltpu.SemaphoreType.DMA((2, chips)),
            pltpu.SemaphoreType.DMA((2,)),
            pltpu.SemaphoreType.DMA((2, chips)),
        ],
        compiler_params=pltpu.CompilerParams(collective_id=2, has_side_effects=True, vmem_limit_bytes=VMEM_LIMIT),
    )(both, w_in, w_out)


def rms_parts(values):
    inverse = lax.rsqrt(jnp.mean(values * values, axis=-1, keepdims=True) + EPS)
    return (values * inverse, inverse)


def rms_back(grad_normed, normed, inverse):
    return inverse * (grad_normed - normed * jnp.mean(grad_normed * normed, axis=-1, keepdims=True))


def spread_offsets(per_offset, block_rows, columns):
    heads_here = per_offset.shape[0]
    period = block_rows + columns
    padded = jnp.pad(per_offset, ((0, 0), (0, 1)))
    tiled = jnp.tile(padded, (1, block_rows))[:, : block_rows * (period - 1)]
    return tiled.reshape(heads_here, block_rows, period - 1)[:, :, block_rows - 1 :]


def offset_sums(grid):
    heads_here, block_rows, columns = grid.shape
    period = block_rows + columns
    widened = jnp.pad(grid, ((0, 0), (0, 0), (block_rows - 1, 0)))
    flat_grid = widened.reshape(heads_here, block_rows * (period - 1))
    flat_grid = jnp.pad(flat_grid, ((0, 0), (0, block_rows)))
    return jnp.sum(flat_grid.reshape(heads_here, block_rows, period), axis=1)[:, : period - 1]


def heads_of(matrix):
    return matrix.reshape(matrix.shape[0], -1, HEAD_DIM)


def local(
    devices_along_shard, tokens_in, w_query, w_key, w_value, output_weight, gain_attn, gain_moe, router_weight,
    bias_table, w_expert_in, w_expert_out, expert_id, slot_id, bucket_id, cotangent,
):
    bits = devices_along_shard.bit_length() - 1
    devices = 2 * devices_along_shard
    seq = lax.axis_index("seq")
    rows, width = w_query.shape
    experts = router_weight.shape[1]
    tokens_here = tokens_in.shape[1]
    length = 2 * tokens_here
    capacity = 2 * max(1, 5 * tokens_here // (8 * experts))
    slots = round_up(capacity, 8)
    pack_rows = round_up(4 * rows + 1, 16)
    heads_side, buckets = bias_table.shape

    extra = jnp.concatenate([router_weight.reshape(-1), gain_attn, gain_moe])
    extra = jnp.pad(extra, (0, width - extra.shape[0]))[None]
    pack = jnp.concatenate([w_query, w_key, w_value, output_weight, extra], axis=0)
    pack = jnp.pad(pack, ((0, pack_rows - pack.shape[0]), (0, 0)))
    table_tile = jnp.pad(bias_table, ((0, 16 - heads_side), (0, 128 - buckets)))
    gathered, both_tokens, both_tables = gather_all(pack, tokens_in[0], table_tile, bits)
    gathered = gathered.reshape(devices, pack_rows, width)
    full_query, full_key, full_value, full_output = (
        gathered[:, n * rows : (n + 1) * rows].reshape(width, width) for n in range(4)
    )
    extra = gathered[:, 4 * rows]
    cut = rows * experts
    full_router = extra[:, :cut].reshape(width, experts)
    full_gain_attn = extra[:, cut : cut + rows].reshape(width).astype(F32)
    full_gain_moe = extra[:, cut + rows : cut + 2 * rows].reshape(width).astype(F32)
    full_table = both_tables[:, :heads_side, :buckets].reshape(2 * heads_side, buckets)

    def mine(array):
        return lax.dynamic_slice_in_dim(array, seq * tokens_here, tokens_here, 0)

    inputs = tokens_in[0].astype(F32)
    normed_all, _ = rms_parts(both_tokens.reshape(length, width).astype(F32))
    normed_attn, inverse_attn = rms_parts(inputs)
    hidden_all = (normed_all * full_gain_attn).astype(BF16)
    hidden_own = (normed_attn * full_gain_attn).astype(BF16)
    queries = heads_of(jnp.dot(hidden_own, full_query, preferred_element_type=F32).astype(BF16))
    keys = heads_of(jnp.dot(hidden_all, full_key, preferred_element_type=F32).astype(BF16))
    values = heads_of(jnp.dot(hidden_all, full_value, preferred_element_type=F32).astype(BF16))

    bucket_onehot = (jnp.arange(buckets, dtype=jnp.int32)[:, None] == bucket_id[None, :]).astype(BF16)
    onehot_here = lax.dynamic_slice_in_dim(
        bucket_onehot, tokens_here * (1 - seq), tokens_here + length - 1, 1
    )
    per_offset = jnp.dot(full_table, onehot_here, preferred_element_type=F32)
    scores = jnp.einsum("qhd,khd->hqk", queries, keys, preferred_element_type=F32)
    scores = scores + spread_offsets(per_offset, tokens_here, length)
    weights = jnp.exp(scores - jnp.max(scores, axis=-1, keepdims=True))
    probs = weights / jnp.sum(weights, axis=-1, keepdims=True)
    probs_low = probs.astype(BF16)
    mixed = jnp.einsum("hqk,khd->qhd", probs_low, values, preferred_element_type=F32)
    mixed = mixed.reshape(tokens_here, width).astype(BF16)

    after_attn = inputs + jnp.dot(mixed, full_output, preferred_element_type=F32)
    normed_moe, inverse_moe = rms_parts(after_attn)
    hidden_moe = (normed_moe * full_gain_moe).astype(BF16)
    router_logits = jnp.dot(hidden_moe, full_router, preferred_element_type=F32)
    gate_weights = jnp.exp(router_logits - jnp.max(router_logits, axis=-1, keepdims=True))
    gate_probs = gate_weights / jnp.sum(gate_weights, axis=-1, keepdims=True)
    chosen = (expert_id[0][:, None] == jnp.arange(experts, dtype=jnp.int32)[None, :]).astype(F32)
    picked = jnp.sum(gate_probs * chosen, axis=-1, keepdims=True)
    slot_of = jnp.where(slot_id[0] >= 0, expert_id[0] * slots + slot_id[0], -1)
    dispatch = (slot_of[:, None] == jnp.arange(experts * slots, dtype=jnp.int32)[None, :]).astype(BF16)
    grad_out = cotangent[0].astype(F32)
    scaled = (picked * grad_out).astype(BF16)
    buffer = contract(dispatch, hidden_moe, 0, 0).astype(BF16)
    grad_slots = contract(dispatch, scaled, 0, 0).astype(BF16)
    both = jnp.concatenate(
        [buffer.reshape(experts, slots, width), grad_slots.reshape(experts, slots, width)], axis=1
    )
    returned, kept, leaving = run_experts(both, w_expert_in[0], w_expert_out[0])
    arriving = lax.ppermute(leaving, "seq", [(0, 1), (1, 0)])
    expert_slots, grad_buffer = returned[:, :slots], returned[:, slots:]

    combined = jnp.dot(dispatch, expert_slots.reshape(-1, width), preferred_element_type=F32)
    block_out = after_attn + picked * combined
    grad_picked = jnp.sum(grad_out * combined, axis=-1, keepdims=True)
    grad_gates = chosen * grad_picked
    grad_logits = gate_probs * (grad_gates - jnp.sum(gate_probs * grad_gates, axis=-1, keepdims=True))
    grad_logits = grad_logits.astype(BF16)
    grad_router = contract(hidden_moe, grad_logits, 0, 0)
    grad_hidden_moe = contract(grad_logits, full_router, 1, 1)
    grad_hidden_moe = grad_hidden_moe + jnp.dot(
        dispatch, grad_buffer.reshape(-1, width), preferred_element_type=F32
    )
    grad_gain_moe = jnp.sum(grad_hidden_moe * normed_moe, axis=0)
    grad_mid = grad_out + rms_back(grad_hidden_moe * full_gain_moe, normed_moe, inverse_moe)
    grad_branch = grad_mid.astype(BF16)
    grad_output = contract(mixed, grad_branch, 0, 0)
    grad_mixed = heads_of(contract(grad_branch, full_output, 1, 1).astype(BF16))

    grad_probs = jnp.einsum("qhd,khd->hqk", grad_mixed, values, preferred_element_type=F32)
    centre = jnp.sum(probs * grad_probs, axis=-1, keepdims=True)
    grad_scores = (probs * (grad_probs - centre)).astype(BF16)
    grad_q = jnp.einsum("hqk,khd->qhd", grad_scores, keys, preferred_element_type=F32)
    grad_k = jnp.einsum("hqk,qhd->khd", grad_scores, queries, preferred_element_type=F32)
    grad_v = jnp.einsum("hqk,qhd->khd", probs_low, grad_mixed, preferred_element_type=F32)
    grad_q = grad_q.reshape(tokens_here, width).astype(BF16)
    grad_k = grad_k.reshape(length, width).astype(BF16)
    grad_v = grad_v.reshape(length, width).astype(BF16)
    grad_offset = offset_sums(grad_scores.astype(F32))
    grad_table = jnp.einsum(
        "ho,bo->hb", grad_offset, onehot_here.astype(F32), precision=lax.Precision.HIGHEST
    )
    grad_table = jnp.pad(grad_table, ((0, 16 - 2 * heads_side), (0, 128 - buckets)))

    back_query = contract(grad_q, full_query, 1, 1)
    back_all = contract(grad_k, full_key, 1, 1) + contract(grad_v, full_value, 1, 1)
    grad_gain_attn = jnp.sum(back_query * normed_attn, axis=0) + jnp.sum(back_all * normed_all, axis=0)
    far = lax.dynamic_slice_in_dim(back_all, (1 - seq) * tokens_here, tokens_here, 0).astype(BF16)

    def by_device(matrix):
        return matrix.reshape(devices, rows, width).astype(BF16)

    extra = jnp.concatenate(
        [
            grad_router.reshape(devices, rows * experts),
            grad_gain_attn.reshape(devices, rows),
            grad_gain_moe.reshape(devices, rows),
        ],
        axis=1,
    )
    extra = jnp.pad(extra, ((0, 0), (0, width - extra.shape[1])))[:, None].astype(BF16)
    pieces = [
        by_device(contract(hidden_own, grad_q, 0, 0)),
        by_device(contract(hidden_all, grad_k, 0, 0)),
        by_device(contract(hidden_all, grad_v, 0, 0)),
        by_device(grad_output),
        extra,
    ]
    blocks = jnp.concatenate(pieces, axis=1)
    blocks = jnp.pad(blocks, ((0, 0), (0, pack_rows - blocks.shape[1]), (0, 0)))
    blocks = blocks.reshape((2,) * (bits + 1) + blocks.shape[1:])
    total, table_sum, far_sum = reduce_all(blocks, grad_table, far, bits)
    share = total[4 * rows]

    grad_hidden_attn = back_query + mine(back_all) + far_sum.astype(F32)
    grad_tokens = grad_mid + rms_back(grad_hidden_attn * full_gain_attn, normed_attn, inverse_attn)
    expert_sum = kept.astype(F32) + arriving.astype(F32)
    return (
        block_out.astype(BF16)[None],
        grad_tokens[None],
        total[:rows],
        total[rows : 2 * rows],
        total[2 * rows : 3 * rows],
        total[3 * rows : 4 * rows],
        share[cut : cut + rows],
        share[cut + rows : cut + 2 * rows],
        share[:cut].reshape(rows, experts),
        lax.dynamic_slice_in_dim(table_sum[:, :buckets], seq * heads_side, heads_side, 0),
        expert_sum[0][None],
        expert_sum[1][None],
    )


def solution(mesh):
    return jax.shard_map(
        functools.partial(local, mesh.shape["shard"]),
        mesh=mesh,
        in_specs=(
            P("shard", "seq", None),
            P(("seq", "shard"), None),
            P(("seq", "shard"), None),
            P(("seq", "shard"), None),
            P(("seq", "shard"), None),
            P(("seq", "shard")),
            P(("seq", "shard")),
            P(("seq", "shard"), None),
            P("seq", None),
            P("shard", None, None),
            P("shard", None, None),
            P("shard", "seq"),
            P("shard", "seq"),
            P(),
            P("shard", "seq", None),
        ),
        out_specs=(
            P("shard", "seq", None),
            P("shard", "seq", None),
            P(("seq", "shard"), None),
            P(("seq", "shard"), None),
            P(("seq", "shard"), None),
            P(("seq", "shard"), None),
            P(("seq", "shard")),
            P(("seq", "shard")),
            P(("seq", "shard"), None),
            P("seq", None),
            P("shard", None, "seq"),
            P("shard", "seq", None),
        ),
        check_vma=False,
    )
```

```python
import functools

import jax
import jax.numpy as jnp
from jax import lax
from jax.experimental import pallas as pl
from jax.experimental.pallas import tpu as pltpu
from jax.sharding import PartitionSpec as P

HEAD_DIM = 64
EPS = 1e-06
MESH = pl.DeviceIdType.MESH
VMEM_LIMIT = 56 * 1024 * 1024
BF16 = jnp.bfloat16
F32 = jnp.float32


def round_up(value, step):
    return (value + step - 1) // step * step


def coordinates(bits):
    shard = lax.axis_index("shard")
    return [lax.axis_index("seq")] + [(shard // 2**b) % 2 for b in reversed(range(bits))]


def partner(dim, bits):
    seq, shard = lax.axis_index("seq"), lax.axis_index("shard")
    if dim == 0:
        return (1 - seq, shard)
    step = 2 ** (bits - dim)
    return (seq, shard + (1 - 2 * ((shard // step) % 2)) * step)


def greet(targets):
    barrier = pltpu.get_barrier_semaphore()
    for target in targets:
        pl.semaphore_signal(barrier, inc=1, device_id=target, device_id_type=MESH)
    pl.semaphore_wait(barrier, len(targets))


def gather_plan(rows, bits):
    far, near = list(range(1, bits - 1)), bits - 1
    orders = [far + [near, 0, bits], far + [0, near, bits]]
    size = 32 if rows > 64 else rows
    starts = range(0, rows, size)
    return [(start, min(size, rows - start), orders[n % 2]) for n, start in enumerate(starts)]


def gather_kernel(bits, plan, pack_ref, tok_ref, table_ref, out_ref, toks_ref, tables_ref, local_sem, send_sem, recv_sem, tok_sem):
    coords = coordinates(bits)
    dims = bits + 1
    greet([partner(d, bits) for d in range(dims)])
    other = partner(0, bits)
    seq = coords[0]
    extras = []
    for n, (src, dst) in enumerate(((tok_ref, toks_ref), (table_ref, tables_ref))):
        copy = pltpu.make_async_remote_copy(
            src, dst.at[seq], tok_sem.at[0, n], tok_sem.at[1, n], device_id=other, device_id_type=MESH
        )
        keep = pltpu.make_async_copy(src, dst.at[seq], tok_sem.at[2, n])
        copy.start()
        keep.start()
        extras += [copy, keep]
    own = pltpu.make_async_copy(pack_ref, out_ref.at[tuple(coords)], local_sem)
    own.start()
    done = [[] for _ in plan]
    flying = [None for _ in plan]
    sent = []
    for step in range(dims):
        for part, (start, rows, order) in enumerate(plan):
            dim = order[step]
            if step == 0:
                src = pack_ref.at[pl.ds(start, rows)]
                dst = out_ref.at[tuple(coords) + (pl.ds(start, rows),)]
            else:
                if step == 1 and part == 0:
                    own.wait()
                flying[part].wait_recv()
                where = tuple(slice(None) if d in done[part] else coords[d] for d in range(dims))
                src = out_ref.at[where + (pl.ds(start, rows),)]
                dst = src
            copy = pltpu.make_async_remote_copy(
                src,
                dst,
                send_sem.at[part, step],
                recv_sem.at[part, step],
                device_id=partner(dim, bits),
                device_id_type=MESH,
            )
            copy.start()
            sent.append(copy)
            flying[part] = copy
            done[part].append(dim)
    for copy in flying:
        copy.wait_recv()
    for copy in sent:
        copy.wait_send()
    for copy in extras:
        copy.wait()


def gather_all(pack, tokens, table, bits):
    rows, columns = pack.shape
    plan = gather_plan(rows, bits)
    lead = (2,) * (bits + 1)
    any_spec = pl.BlockSpec(memory_space=pl.ANY)
    return pl.pallas_call(
        functools.partial(gather_kernel, bits, plan),
        out_shape=(
            jax.ShapeDtypeStruct(lead + (rows, columns), BF16),
            jax.ShapeDtypeStruct((2,) + tokens.shape, BF16),
            jax.ShapeDtypeStruct((2,) + table.shape, BF16),
        ),
        in_specs=[any_spec] * 3,
        out_specs=(any_spec,) * 3,
        scratch_shapes=[
            pltpu.SemaphoreType.DMA,
            pltpu.SemaphoreType.DMA((len(plan), bits + 1)),
            pltpu.SemaphoreType.DMA((len(plan), bits + 1)),
            pltpu.SemaphoreType.DMA((3, 2)),
        ],
        compiler_params=pltpu.CompilerParams(collective_id=0, has_side_effects=True, vmem_limit_bytes=VMEM_LIMIT),
    )(pack, tokens, table)


def reduce_kernel(bits, plan, places, inputs, *refs):
    ins, rest = refs[:inputs], refs[inputs:]
    table_ref, far_ref, out_ref, table_out, far_out, *rest = rest
    parts, dims = len(plan), bits + 1
    rest = list(rest)
    landed = [rest[p * dims : (p + 1) * dims] for p in range(parts)]
    rest = rest[parts * dims :]
    sums = [rest[p * bits : (p + 1) * bits] for p in range(parts)]
    rest = rest[parts * bits :]
    table_landed, table_sums, send_sem, recv_sem, table_sem, far_sem = rest
    coords = coordinates(bits)
    greet([partner(d, bits) for d in range(dims)])
    far_copy = pltpu.make_async_remote_copy(
        far_ref, far_out, far_sem.at[0], far_sem.at[1], device_id=partner(0, bits), device_id_type=MESH
    )
    far_copy.start()
    orders = [list(reversed(order)) for _, _, order in plan]
    held = [
        ins[which].at[(slice(None),) * dims + (pl.ds(start, plan[part][1]),)]
        for part, (which, start) in enumerate(places)
    ]
    left = [list(range(dims)) for _ in range(parts)]
    sent = [far_copy]
    table_now = table_ref
    for step in range(dims):
        flying = []
        for part in range(parts):
            dim = orders[part][step]
            spot = left[part].index(dim)
            whole = (slice(None),) * spot
            copy = pltpu.make_async_remote_copy(
                held[part].at[whole + (1 - coords[dim],)],
                landed[part][step],
                send_sem.at[part, step],
                recv_sem.at[part, step],
                device_id=partner(dim, bits),
                device_id_type=MESH,
            )
            copy.start()
            sent.append(copy)
            flying.append((copy, whole, dim))
        small = pltpu.make_async_remote_copy(
            table_now,
            table_landed.at[step],
            table_sem.at[0, step],
            table_sem.at[1, step],
            device_id=partner(step, bits),
            device_id_type=MESH,
        )
        small.start()
        sent.append(small)
        for part, (copy, whole, dim) in enumerate(flying):
            copy.wait_recv()
            total = held[part][whole + (coords[dim],)].astype(F32) + landed[part][step][...].astype(F32)
            left[part].remove(dim)
            if step == dims - 1:
                out_ref[pl.ds(plan[part][0], plan[part][1])] = total
            else:
                sums[part][step][...] = total.astype(BF16)
                held[part] = sums[part][step]
        small.wait_recv()
        total = table_now[...] + table_landed[step]
        if step == dims - 1:
            table_out[...] = total
        else:
            table_sums[step] = total
            table_now = table_sums.at[step]
    far_copy.wait_recv()
    for copy in sent:
        copy.wait_send()


def reduce_all(blocks, table, far, bits):
    dims = bits + 1
    width = blocks[0].shape[-1]
    rows = sum(block.shape[-2] for block in blocks)
    plan = gather_plan(rows, bits)
    first = blocks[0].shape[-2]
    places = [(0, start) if start < first else (1, start - first) for start, _, _ in plan]
    vmem = pl.BlockSpec(memory_space=pltpu.VMEM)
    count = len(plan)
    scratch = []
    for _, part_rows, _ in plan:
        scratch += [pltpu.VMEM((2,) * (dims - 1 - s) + (part_rows, width), BF16) for s in range(dims)]
    for _, part_rows, _ in plan:
        scratch += [pltpu.VMEM((2,) * (dims - 1 - s) + (part_rows, width), BF16) for s in range(dims - 1)]
    scratch += [
        pltpu.VMEM((dims,) + table.shape, F32),
        pltpu.VMEM((dims,) + table.shape, F32),
        pltpu.SemaphoreType.DMA((count, dims)),
        pltpu.SemaphoreType.DMA((count, dims)),
        pltpu.SemaphoreType.DMA((2, dims)),
        pltpu.SemaphoreType.DMA((2,)),
    ]
    return pl.pallas_call(
        functools.partial(reduce_kernel, bits, plan, places, len(blocks)),
        out_shape=(
            jax.ShapeDtypeStruct((rows, width), F32),
            jax.ShapeDtypeStruct(table.shape, F32),
            jax.ShapeDtypeStruct(far.shape, BF16),
        ),
        in_specs=[vmem] * (len(blocks) + 2),
        out_specs=(vmem,) * 3,
        scratch_shapes=scratch,
        compiler_params=pltpu.CompilerParams(collective_id=1, has_side_effects=True, vmem_limit_bytes=VMEM_LIMIT),
    )(*blocks, table, far)


def contract(a, b, on_a, on_b):
    return lax.dot_general(a, b, (((on_a,), (on_b,)), ((), ())), preferred_element_type=F32)


GELU_SCALE = 0.7978845608028654


def expert_kernel(
    chips, both_ref, w_in_ref, w_out_ref, back_ref, keep_ref, leave_ref,
    rows_ref, x_ref, g_ref, act_ref, gpre_ref, part_ref, sib_ref, ret_ref,
    in_sem, fwd_sem, sib_sem, out_sem,
):
    seq, shard = lax.axis_index("seq"), lax.axis_index("shard")
    chip, core = shard // 2, shard % 2
    sibling = (seq, shard + 1 - 2 * core)
    slots, width = both_ref.shape[1] // 2, both_ref.shape[2]
    hidden = w_in_ref.shape[1]

    def device_of(other):
        return (seq, 2 * other + core)

    greet([device_of((chip + j) % chips) for j in range(1, chips)] + [sibling])
    sent = []
    copies = {}
    for j in range(1, chips):
        to = (chip + j) % chips
        copy = pltpu.make_async_remote_copy(
            both_ref.at[to], rows_ref.at[chip, core], in_sem.at[0, j], in_sem.at[1, j],
            device_id=device_of(to), device_id_type=MESH,
        )
        copy.start()
        copies[j] = copy
        sent.append(copy)
    rows_ref[chip, core] = both_ref[chip]
    forwards = []
    for j in range(chips):
        source = (chip + chips - j) % chips
        if j:
            copies[j].wait_recv()
        copy = pltpu.make_async_remote_copy(
            rows_ref.at[source, core], rows_ref.at[source, core], fwd_sem.at[0, j], fwd_sem.at[1, j],
            device_id=sibling, device_id_type=MESH,
        )
        copy.start()
        forwards.append(copy)
        sent.append(copy)
    for copy in forwards:
        copy.wait_recv()

    group = chips
    while group * 2 * slots > 512:
        group //= 2
    block = group * 2 * slots
    piece = 512

    @pl.loop(0, chips // group)
    def _(t):
        rows = rows_ref[pl.ds(t * group, group)].astype(F32)
        x = rows[:, :, :slots].reshape(block, width).astype(BF16)
        g = rows[:, :, slots:].reshape(block, width).astype(BF16)
        out_sum = jnp.zeros((block, width), F32)
        half_sum = jnp.zeros((block, width), F32)
        where = pl.ds(pl.multiple_of(t * block, block), block)
        x_ref[where] = x
        g_ref[where] = g
        for h in range(hidden // piece):
            cols = pl.ds(h * piece, piece)
            pre = jnp.dot(x, w_in_ref[:, cols], preferred_element_type=F32)
            gact = contract(g, w_out_ref[cols, :], 1, 1)
            square = pre * pre
            t_val = jnp.tanh(GELU_SCALE * (pre + 0.044715 * square * pre))
            act = (0.5 * pre * (1.0 + t_val)).astype(BF16)
            slope = 0.5 * (1.0 + t_val) + 0.5 * pre * (1.0 - t_val * t_val) * (
                GELU_SCALE * (1.0 + 0.134145 * square)
            )
            gpre = (gact * slope).astype(BF16)
            act_ref[where, cols] = act
            gpre_ref[where, cols] = gpre
            out_sum += jnp.dot(act, w_out_ref[cols, :], preferred_element_type=F32)
            half_sum += contract(gpre, w_in_ref[:, cols], 1, 1)
        out_sum = out_sum.reshape(group, 2, slots, width)
        half_sum = half_sum.reshape(group, 2, slots, width)
        both = jnp.concatenate([out_sum, half_sum], axis=2).astype(BF16)
        for u in range(2):
            part_ref[u, pl.ds(t * group, group)] = both[:, u]

    swap = pltpu.make_async_remote_copy(
        part_ref.at[1 - core], sib_ref, sib_sem.at[0], sib_sem.at[1], device_id=sibling, device_id_type=MESH
    )
    swap.start()
    sent.append(swap)
    side = hidden // 2
    away = pl.ds(pl.multiple_of((1 - seq) * side, side), side)
    home = pl.ds(pl.multiple_of(seq * side, side), side)
    returns = []
    swap.wait_recv()
    ret_ref[...] = (part_ref[core].astype(F32) + sib_ref[...].astype(F32)).astype(BF16)
    for j in range(1, chips):
        to = (chip + j) % chips
        copy = pltpu.make_async_remote_copy(
            ret_ref.at[to], back_ref.at[chip], out_sem.at[0, j], out_sem.at[1, j],
            device_id=device_of(to), device_id_type=MESH,
        )
        copy.start()
        returns.append(copy)
        sent.append(copy)
    back_ref[chip] = ret_ref[chip]
    for target, cols in ((leave_ref, away), (keep_ref, home)):
        target[0] = contract(x_ref[...], gpre_ref[:, cols], 0, 0).astype(BF16)
        target[1] = contract(act_ref[:, cols], g_ref[...], 0, 0).astype(BF16)
    for copy in returns:
        copy.wait_recv()
    for copy in sent:
        copy.wait_send()


def run_experts(both, w_in, w_out):
    chips, doubled, width = both.shape
    hidden = w_in.shape[1]
    rows = chips * doubled
    vmem = pl.BlockSpec(memory_space=pltpu.VMEM)
    half = jax.ShapeDtypeStruct((2, width, hidden // 2), BF16)
    return pl.pallas_call(
        functools.partial(expert_kernel, chips),
        out_shape=(jax.ShapeDtypeStruct(both.shape, BF16), half, half),
        in_specs=[vmem] * 3,
        out_specs=(vmem,) * 3,
        scratch_shapes=[
            pltpu.VMEM((chips, 2, doubled, width), BF16),
            pltpu.VMEM((rows, width), BF16),
            pltpu.VMEM((rows, width), BF16),
            pltpu.VMEM((rows, hidden), BF16),
            pltpu.VMEM((rows, hidden), BF16),
            pltpu.VMEM((2, chips, doubled, width), BF16),
            pltpu.VMEM((chips, doubled, width), BF16),
            pltpu.VMEM((chips, doubled, width), BF16),
            pltpu.SemaphoreType.DMA((2, chips)),
            pltpu.SemaphoreType.DMA((2, chips)),
            pltpu.SemaphoreType.DMA((2,)),
            pltpu.SemaphoreType.DMA((2, chips)),
        ],
        compiler_params=pltpu.CompilerParams(collective_id=2, has_side_effects=True, vmem_limit_bytes=VMEM_LIMIT),
    )(both, w_in, w_out)


def rms_parts(values):
    inverse = lax.rsqrt(jnp.mean(values * values, axis=-1, keepdims=True) + EPS)
    return (values * inverse, inverse)


def rms_back(grad_normed, normed, inverse):
    return inverse * (grad_normed - normed * jnp.mean(grad_normed * normed, axis=-1, keepdims=True))


def attend_kernel(own_ref, all_ref, wq_ref, wk_ref, wv_ref, offset_ref, q_ref, k_ref, v_ref, probs_ref, mixed_ref):
    own, every = own_ref[...], all_ref[...]
    q_ref[...] = jnp.dot(own, wq_ref[...], preferred_element_type=F32).astype(BF16)
    k_ref[...] = jnp.dot(every, wk_ref[...], preferred_element_type=F32).astype(BF16)
    v_ref[...] = jnp.dot(every, wv_ref[...], preferred_element_type=F32).astype(BF16)
    here, length = own.shape[0], every.shape[0]
    period = offset_ref.shape[1]
    for pair in range(probs_ref.shape[0] // 2):
        cols = pl.ds(2 * HEAD_DIM * pair, 2 * HEAD_DIM)
        q, k, v = q_ref[:, cols], k_ref[:, cols], v_ref[:, cols]
        mixed = []
        for side in range(2):
            head = 2 * pair + side
            part = slice(side * HEAD_DIM, (side + 1) * HEAD_DIM)
            line = jnp.broadcast_to(offset_ref[head : head + 1, :], (here, period))
            bias = pltpu.roll(line, period - here + 1, 1, stride=1, stride_axis=0)[:, :length]
            scores = contract(q[:, part], k[:, part], 1, 1) + bias
            weights = jnp.exp(scores - jnp.max(scores, axis=-1, keepdims=True))
            probs = weights / jnp.sum(weights, axis=-1, keepdims=True)
            probs_ref[head] = probs
            mixed.append(jnp.dot(probs.astype(BF16), v[:, part], preferred_element_type=F32))
        mixed_ref[:, cols] = jnp.concatenate(mixed, axis=1).astype(BF16)


def attend(own, every, wq, wk, wv, per_offset, heads):
    vmem = pl.BlockSpec(memory_space=pltpu.VMEM)
    low_own = jax.ShapeDtypeStruct(own.shape, BF16)
    low_all = jax.ShapeDtypeStruct(every.shape, BF16)
    probs = jax.ShapeDtypeStruct((heads, own.shape[0], every.shape[0]), F32)
    return pl.pallas_call(
        attend_kernel,
        out_shape=(low_own, low_all, low_all, probs, low_own),
        in_specs=[vmem] * 6,
        out_specs=(vmem,) * 5,
        compiler_params=pltpu.CompilerParams(vmem_limit_bytes=VMEM_LIMIT),
    )(own, every, wq, wk, wv, per_offset)


def attend_back_kernel(
    devices, own_ref, all_ref, wq_ref, wk_ref, wv_ref, wo_ref, q_ref, k_ref, v_ref, probs_ref, mixed_ref, branch_ref,
    main_ref, back_own_ref, back_all_ref, offset_ref, gq_ref, gk_ref, gv_ref, gm_ref,
):
    here, length = own_ref.shape[0], all_ref.shape[0]
    width = own_ref.shape[1]
    period = offset_ref.shape[1]
    branch = branch_ref[...]
    gm_ref[...] = contract(branch, wo_ref[...], 1, 1).astype(BF16)
    down = lax.broadcasted_iota(jnp.int32, (here, here), 0)
    across = lax.broadcasted_iota(jnp.int32, (here, here), 1)
    flip = jnp.where(down + across == here - 1, 1.0, 0.0).astype(BF16)
    offset_ref[...] = jnp.zeros_like(offset_ref)
    for pair in range(probs_ref.shape[0] // 2):
        cols = pl.ds(2 * HEAD_DIM * pair, 2 * HEAD_DIM)
        q, k, v, gm = q_ref[:, cols], k_ref[:, cols], v_ref[:, cols], gm_ref[:, cols]
        grads = [[], [], []]
        for side in range(2):
            head = 2 * pair + side
            part = slice(side * HEAD_DIM, (side + 1) * HEAD_DIM)
            probs = probs_ref[head]
            grad_probs = contract(gm[:, part], v[:, part], 1, 1)
            centre = jnp.sum(probs * grad_probs, axis=-1, keepdims=True)
            scores = (probs * (grad_probs - centre)).astype(BF16)
            grads[0].append(jnp.dot(scores, k[:, part], preferred_element_type=F32))
            grads[1].append(contract(scores, q[:, part], 0, 0))
            grads[2].append(contract(probs.astype(BF16), gm[:, part], 0, 0))
            turned = jnp.dot(flip, scores, preferred_element_type=F32)
            turned = jnp.concatenate([turned, jnp.zeros((here, period - length), F32)], axis=1)
            turned = pltpu.roll(turned, 0, 1, stride=1, stride_axis=0)
            offset_ref[head : head + 1, :] = jnp.sum(turned, axis=0, keepdims=True)
        for ref, halves in zip((gq_ref, gk_ref, gv_ref), grads):
            ref[:, cols] = jnp.concatenate(halves, axis=1).astype(BF16)
    gq, gk, gv = gq_ref[...], gk_ref[...], gv_ref[...]
    back_own_ref[...] = contract(gq, wq_ref[...], 1, 1)
    back_all_ref[...] = contract(gk, wk_ref[...], 1, 1) + contract(gv, wv_ref[...], 1, 1)
    pairs = (
        ((own_ref, gq), (all_ref, gk)),
        ((all_ref, gv), (mixed_ref, branch)),
    )
    if main_ref.shape[0] == devices:
        rows = width // devices
        for n, some in enumerate(pairs):
            both = [contract(left[...], right, 0, 0).reshape(devices, rows, width) for left, right in some]
            main_ref[:, pl.ds(2 * rows * n, 2 * rows)] = jnp.concatenate(both, axis=1).astype(BF16)
    else:
        for n, some in enumerate(pairs):
            for m, (left, right) in enumerate(some):
                main_ref[2 * n + m] = contract(left[...], right, 0, 0).astype(BF16)


def attend_back(devices, own, every, wq, wk, wv, wo, q, k, v, probs, mixed, branch, packed):
    vmem = pl.BlockSpec(memory_space=pltpu.VMEM)
    here, width = own.shape
    length = every.shape[0]
    main = (devices, 4 * (width // devices), width) if packed else (4, width, width)
    return pl.pallas_call(
        functools.partial(attend_back_kernel, devices),
        out_shape=(
            jax.ShapeDtypeStruct(main, BF16),
            jax.ShapeDtypeStruct((here, width), F32),
            jax.ShapeDtypeStruct((length, width), F32),
            jax.ShapeDtypeStruct((16, here + length), F32),
        ),
        in_specs=[vmem] * 12,
        out_specs=(vmem,) * 4,
        scratch_shapes=[
            pltpu.VMEM((here, width), BF16),
            pltpu.VMEM((length, width), BF16),
            pltpu.VMEM((length, width), BF16),
            pltpu.VMEM((here, width), BF16),
        ],
        compiler_params=pltpu.CompilerParams(vmem_limit_bytes=VMEM_LIMIT),
    )(own, every, wq, wk, wv, wo, q, k, v, probs, mixed, branch)


def local(
    devices_along_shard, tokens_in, w_query, w_key, w_value, output_weight, gain_attn, gain_moe, router_weight,
    bias_table, w_expert_in, w_expert_out, expert_id, slot_id, bucket_id, cotangent,
):
    bits = devices_along_shard.bit_length() - 1
    devices = 2 * devices_along_shard
    seq = lax.axis_index("seq")
    rows, width = w_query.shape
    experts = router_weight.shape[1]
    tokens_here = tokens_in.shape[1]
    length = 2 * tokens_here
    capacity = 2 * max(1, 5 * tokens_here // (8 * experts))
    slots = round_up(capacity, 8)
    pack_rows = round_up(4 * rows + 1, 16)
    heads_side, buckets = bias_table.shape

    extra = jnp.concatenate([router_weight.reshape(-1), gain_attn, gain_moe])
    extra = jnp.pad(extra, (0, width - extra.shape[0]))[None]
    pack = jnp.concatenate([w_query, w_key, w_value, output_weight, extra], axis=0)
    pack = jnp.pad(pack, ((0, pack_rows - pack.shape[0]), (0, 0)))
    table_tile = jnp.pad(bias_table, ((0, 16 - heads_side), (0, 128 - buckets)))
    gathered, both_tokens, both_tables = gather_all(pack, tokens_in[0], table_tile, bits)
    gathered = gathered.reshape(devices, pack_rows, width)
    full_query, full_key, full_value, full_output = (
        gathered[:, n * rows : (n + 1) * rows].reshape(width, width) for n in range(4)
    )
    extra = gathered[:, 4 * rows]
    cut = rows * experts
    full_router = extra[:, :cut].reshape(width, experts)
    full_gain_attn = extra[:, cut : cut + rows].reshape(width).astype(F32)
    full_gain_moe = extra[:, cut + rows : cut + 2 * rows].reshape(width).astype(F32)
    full_table = both_tables[:, :heads_side, :buckets].reshape(2 * heads_side, buckets)

    def mine(array):
        return lax.dynamic_slice_in_dim(array, seq * tokens_here, tokens_here, 0)

    inputs = tokens_in[0].astype(F32)
    normed_all, _ = rms_parts(both_tokens.reshape(length, width).astype(F32))
    normed_attn, inverse_attn = rms_parts(inputs)
    hidden_all = (normed_all * full_gain_attn).astype(BF16)
    hidden_own = (normed_attn * full_gain_attn).astype(BF16)
    bucket_onehot = (jnp.arange(buckets, dtype=jnp.int32)[:, None] == bucket_id[None, :]).astype(BF16)
    onehot_here = lax.dynamic_slice_in_dim(
        bucket_onehot, tokens_here * (1 - seq), tokens_here + length - 1, 1
    )
    onehot_here = jnp.pad(onehot_here, ((0, 0), (0, 1)))
    heads = 2 * heads_side
    per_offset = jnp.dot(
        jnp.pad(full_table, ((0, 16 - heads), (0, 0))), onehot_here, preferred_element_type=F32
    )
    queries, keys, values, probs, mixed = attend(
        hidden_own, hidden_all, full_query, full_key, full_value, per_offset, heads
    )

    after_attn = inputs + jnp.dot(mixed, full_output, preferred_element_type=F32)
    normed_moe, inverse_moe = rms_parts(after_attn)
    hidden_moe = (normed_moe * full_gain_moe).astype(BF16)
    router_logits = jnp.dot(hidden_moe, full_router, preferred_element_type=F32)
    gate_weights = jnp.exp(router_logits - jnp.max(router_logits, axis=-1, keepdims=True))
    gate_probs = gate_weights / jnp.sum(gate_weights, axis=-1, keepdims=True)
    chosen = (expert_id[0][:, None] == jnp.arange(experts, dtype=jnp.int32)[None, :]).astype(F32)
    picked = jnp.sum(gate_probs * chosen, axis=-1, keepdims=True)
    slot_of = jnp.where(slot_id[0] >= 0, expert_id[0] * slots + slot_id[0], -1)
    dispatch = (slot_of[:, None] == jnp.arange(experts * slots, dtype=jnp.int32)[None, :]).astype(BF16)
    grad_out = cotangent[0].astype(F32)
    scaled = (picked * grad_out).astype(BF16)
    buffer = contract(dispatch, hidden_moe, 0, 0).astype(BF16)
    grad_slots = contract(dispatch, scaled, 0, 0).astype(BF16)
    both = jnp.concatenate(
        [buffer.reshape(experts, slots, width), grad_slots.reshape(experts, slots, width)], axis=1
    )
    returned, kept, leaving = run_experts(both, w_expert_in[0], w_expert_out[0])
    arriving = lax.ppermute(leaving, "seq", [(0, 1), (1, 0)])
    expert_slots, grad_buffer = returned[:, :slots], returned[:, slots:]

    combined = jnp.dot(dispatch, expert_slots.reshape(-1, width), preferred_element_type=F32)
    block_out = after_attn + picked * combined
    grad_picked = jnp.sum(grad_out * combined, axis=-1, keepdims=True)
    grad_gates = chosen * grad_picked
    grad_logits = gate_probs * (grad_gates - jnp.sum(gate_probs * grad_gates, axis=-1, keepdims=True))
    grad_logits = grad_logits.astype(BF16)
    grad_router = contract(hidden_moe, grad_logits, 0, 0)
    grad_hidden_moe = contract(grad_logits, full_router, 1, 1)
    grad_hidden_moe = grad_hidden_moe + jnp.dot(
        dispatch, grad_buffer.reshape(-1, width), preferred_element_type=F32
    )
    grad_gain_moe = jnp.sum(grad_hidden_moe * normed_moe, axis=0)
    grad_mid = grad_out + rms_back(grad_hidden_moe * full_gain_moe, normed_moe, inverse_moe)
    grad_branch = grad_mid.astype(BF16)
    packed = rows % 8 == 0
    main, back_query, back_all, grad_offset = attend_back(
        devices, hidden_own, hidden_all, full_query, full_key, full_value, full_output,
        queries, keys, values, probs, mixed, grad_branch, packed,
    )
    grad_table = jnp.einsum(
        "ho,bo->hb", grad_offset, onehot_here.astype(F32), precision=lax.Precision.HIGHEST
    )
    grad_table = jnp.pad(grad_table, ((0, 0), (0, 128 - buckets)))
    grad_gain_attn = jnp.sum(back_query * normed_attn, axis=0) + jnp.sum(back_all * normed_all, axis=0)
    far = lax.dynamic_slice_in_dim(back_all, (1 - seq) * tokens_here, tokens_here, 0).astype(BF16)

    extra = jnp.concatenate(
        [
            grad_router.reshape(devices, rows * experts),
            grad_gain_attn.reshape(devices, rows),
            grad_gain_moe.reshape(devices, rows),
        ],
        axis=1,
    )
    extra = jnp.pad(extra, ((0, 0), (0, width - extra.shape[1])))[:, None].astype(BF16)
    if packed:
        blocks = [main, jnp.pad(extra, ((0, 0), (0, pack_rows - 4 * rows - 1), (0, 0)))]
    else:
        joined = jnp.concatenate([main[n].reshape(devices, rows, width) for n in range(4)] + [extra], axis=1)
        blocks = [jnp.pad(joined, ((0, 0), (0, pack_rows - joined.shape[1]), (0, 0)))]
    blocks = [block.reshape((2,) * (bits + 1) + block.shape[1:]) for block in blocks]
    total, table_sum, far_sum = reduce_all(blocks, grad_table, far, bits)
    share = total[4 * rows]

    grad_hidden_attn = back_query + mine(back_all) + far_sum.astype(F32)
    grad_tokens = grad_mid + rms_back(grad_hidden_attn * full_gain_attn, normed_attn, inverse_attn)
    expert_sum = kept.astype(F32) + arriving.astype(F32)
    return (
        block_out.astype(BF16)[None],
        grad_tokens[None],
        total[:rows],
        total[rows : 2 * rows],
        total[2 * rows : 3 * rows],
        total[3 * rows : 4 * rows],
        share[cut : cut + rows],
        share[cut + rows : cut + 2 * rows],
        share[:cut].reshape(rows, experts),
        lax.dynamic_slice_in_dim(table_sum[:, :buckets], seq * heads_side, heads_side, 0),
        expert_sum[0][None],
        expert_sum[1][None],
    )


def solution(mesh):
    return jax.shard_map(
        functools.partial(local, mesh.shape["shard"]),
        mesh=mesh,
        in_specs=(
            P("shard", "seq", None),
            P(("seq", "shard"), None),
            P(("seq", "shard"), None),
            P(("seq", "shard"), None),
            P(("seq", "shard"), None),
            P(("seq", "shard")),
            P(("seq", "shard")),
            P(("seq", "shard"), None),
            P("seq", None),
            P("shard", None, None),
            P("shard", None, None),
            P("shard", "seq"),
            P("shard", "seq"),
            P(),
            P("shard", "seq", None),
        ),
        out_specs=(
            P("shard", "seq", None),
            P("shard", "seq", None),
            P(("seq", "shard"), None),
            P(("seq", "shard"), None),
            P(("seq", "shard"), None),
            P(("seq", "shard"), None),
            P(("seq", "shard")),
            P(("seq", "shard")),
            P(("seq", "shard"), None),
            P("seq", None),
            P("shard", None, "seq"),
            P("shard", "seq", None),
        ),
        check_vma=False,
    )
```

```python
import functools

import jax
import jax.numpy as jnp
from jax import lax
from jax.experimental import pallas as pl
from jax.experimental.pallas import tpu as pltpu
from jax.sharding import PartitionSpec as P

HEAD_DIM = 64
EPS = 1e-06
MESH = pl.DeviceIdType.MESH
VMEM_LIMIT = 56 * 1024 * 1024
BF16 = jnp.bfloat16
F32 = jnp.float32


def round_up(value, step):
    return (value + step - 1) // step * step


def coordinates(bits):
    shard = lax.axis_index("shard")
    return [lax.axis_index("seq")] + [(shard // 2**b) % 2 for b in reversed(range(bits))]


def partner(dim, bits):
    seq, shard = lax.axis_index("seq"), lax.axis_index("shard")
    if dim == 0:
        return (1 - seq, shard)
    step = 2 ** (bits - dim)
    return (seq, shard + (1 - 2 * ((shard // step) % 2)) * step)


def greet(targets):
    barrier = pltpu.get_barrier_semaphore()
    for target in targets:
        pl.semaphore_signal(barrier, inc=1, device_id=target, device_id_type=MESH)
    pl.semaphore_wait(barrier, len(targets))


def gather_plan(rows, bits):
    far, near = list(range(1, bits - 1)), bits - 1
    orders = [far + [near, 0, bits], far + [0, near, bits]]
    size = 32 if rows > 64 else rows
    starts = range(0, rows, size)
    return [(start, min(size, rows - start), orders[n % 2]) for n, start in enumerate(starts)]


def gather_kernel(bits, plan, pack_ref, tok_ref, table_ref, out_ref, toks_ref, tables_ref, local_sem, send_sem, recv_sem, tok_sem):
    coords = coordinates(bits)
    dims = bits + 1
    greet([partner(d, bits) for d in range(dims)])
    other = partner(0, bits)
    seq = coords[0]
    extras = []
    for n, (src, dst) in enumerate(((tok_ref, toks_ref), (table_ref, tables_ref))):
        copy = pltpu.make_async_remote_copy(
            src, dst.at[seq], tok_sem.at[0, n], tok_sem.at[1, n], device_id=other, device_id_type=MESH
        )
        keep = pltpu.make_async_copy(src, dst.at[seq], tok_sem.at[2, n])
        copy.start()
        keep.start()
        extras += [copy, keep]
    own = pltpu.make_async_copy(pack_ref, out_ref.at[tuple(coords)], local_sem)
    own.start()
    done = [[] for _ in plan]
    flying = [None for _ in plan]
    sent = []
    for step in range(dims):
        for part, (start, rows, order) in enumerate(plan):
            dim = order[step]
            if step == 0:
                src = pack_ref.at[pl.ds(start, rows)]
                dst = out_ref.at[tuple(coords) + (pl.ds(start, rows),)]
            else:
                if step == 1 and part == 0:
                    own.wait()
                flying[part].wait_recv()
                where = tuple(slice(None) if d in done[part] else coords[d] for d in range(dims))
                src = out_ref.at[where + (pl.ds(start, rows),)]
                dst = src
            copy = pltpu.make_async_remote_copy(
                src,
                dst,
                send_sem.at[part, step],
                recv_sem.at[part, step],
                device_id=partner(dim, bits),
                device_id_type=MESH,
            )
            copy.start()
            sent.append(copy)
            flying[part] = copy
            done[part].append(dim)
    for copy in flying:
        copy.wait_recv()
    for copy in sent:
        copy.wait_send()
    for copy in extras:
        copy.wait()


def gather_all(pack, tokens, table, bits):
    rows, columns = pack.shape
    plan = gather_plan(rows, bits)
    lead = (2,) * (bits + 1)
    any_spec = pl.BlockSpec(memory_space=pl.ANY)
    return pl.pallas_call(
        functools.partial(gather_kernel, bits, plan),
        out_shape=(
            jax.ShapeDtypeStruct(lead + (rows, columns), BF16),
            jax.ShapeDtypeStruct((2,) + tokens.shape, BF16),
            jax.ShapeDtypeStruct((2,) + table.shape, BF16),
        ),
        in_specs=[any_spec] * 3,
        out_specs=(any_spec,) * 3,
        scratch_shapes=[
            pltpu.SemaphoreType.DMA,
            pltpu.SemaphoreType.DMA((len(plan), bits + 1)),
            pltpu.SemaphoreType.DMA((len(plan), bits + 1)),
            pltpu.SemaphoreType.DMA((3, 2)),
        ],
        compiler_params=pltpu.CompilerParams(collective_id=0, has_side_effects=True, vmem_limit_bytes=VMEM_LIMIT),
    )(pack, tokens, table)


def reduce_kernel(bits, plan, places, inputs, *refs):
    ins, rest = refs[:inputs], refs[inputs:]
    table_ref, far_ref, out_ref, table_out, far_out, *rest = rest
    parts, dims = len(plan), bits + 1
    rest = list(rest)
    landed = [rest[p * dims : (p + 1) * dims] for p in range(parts)]
    rest = rest[parts * dims :]
    sums = [rest[p * bits : (p + 1) * bits] for p in range(parts)]
    rest = rest[parts * bits :]
    table_landed, table_sums, send_sem, recv_sem, table_sem, far_sem = rest
    coords = coordinates(bits)
    greet([partner(d, bits) for d in range(dims)])
    far_copy = pltpu.make_async_remote_copy(
        far_ref, far_out, far_sem.at[0], far_sem.at[1], device_id=partner(0, bits), device_id_type=MESH
    )
    far_copy.start()
    order = list(range(bits, -1, -1))
    held = [
        ins[which].at[(slice(None),) * dims + (pl.ds(start, plan[part][1]),)]
        for part, (which, start) in enumerate(places)
    ]
    left = [list(range(dims)) for _ in range(parts)]
    sent = [far_copy]
    table_now = table_ref
    flying = [None] * parts

    def begin(part, step):
        dim = order[step]
        whole = (slice(None),) * left[part].index(dim)
        copy = pltpu.make_async_remote_copy(
            held[part].at[whole + (1 - coords[dim],)],
            landed[part][step],
            send_sem.at[part, step],
            recv_sem.at[part, step],
            device_id=partner(dim, bits),
            device_id_type=MESH,
        )
        copy.start()
        sent.append(copy)
        flying[part] = (copy, whole, dim)

    for part in range(parts):
        begin(part, 0)
    for step in range(dims):
        small = pltpu.make_async_remote_copy(
            table_now,
            table_landed.at[step],
            table_sem.at[0, step],
            table_sem.at[1, step],
            device_id=partner(step, bits),
            device_id_type=MESH,
        )
        small.start()
        sent.append(small)
        for part in range(parts):
            copy, whole, dim = flying[part]
            copy.wait_recv()
            total = held[part][whole + (coords[dim],)].astype(F32) + landed[part][step][...].astype(F32)
            left[part].remove(dim)
            if step == dims - 1:
                out_ref[pl.ds(plan[part][0], plan[part][1])] = total
            else:
                sums[part][step][...] = total.astype(BF16)
                held[part] = sums[part][step]
                begin(part, step + 1)
        small.wait_recv()
        total = table_now[...] + table_landed[step]
        if step == dims - 1:
            table_out[...] = total
        else:
            table_sums[step] = total
            table_now = table_sums.at[step]
    far_copy.wait_recv()
    for copy in sent:
        copy.wait_send()


def reduce_all(blocks, table, far, bits):
    dims = bits + 1
    width = blocks[0].shape[-1]
    rows = sum(block.shape[-2] for block in blocks)
    plan = gather_plan(rows, bits)
    first = blocks[0].shape[-2]
    places = [(0, start) if start < first else (1, start - first) for start, _, _ in plan]
    vmem = pl.BlockSpec(memory_space=pltpu.VMEM)
    count = len(plan)
    scratch = []
    for _, part_rows, _ in plan:
        scratch += [pltpu.VMEM((2,) * (dims - 1 - s) + (part_rows, width), BF16) for s in range(dims)]
    for _, part_rows, _ in plan:
        scratch += [pltpu.VMEM((2,) * (dims - 1 - s) + (part_rows, width), BF16) for s in range(dims - 1)]
    scratch += [
        pltpu.VMEM((dims,) + table.shape, F32),
        pltpu.VMEM((dims,) + table.shape, F32),
        pltpu.SemaphoreType.DMA((count, dims)),
        pltpu.SemaphoreType.DMA((count, dims)),
        pltpu.SemaphoreType.DMA((2, dims)),
        pltpu.SemaphoreType.DMA((2,)),
    ]
    return pl.pallas_call(
        functools.partial(reduce_kernel, bits, plan, places, len(blocks)),
        out_shape=(
            jax.ShapeDtypeStruct((rows, width), F32),
            jax.ShapeDtypeStruct(table.shape, F32),
            jax.ShapeDtypeStruct(far.shape, BF16),
        ),
        in_specs=[vmem] * (len(blocks) + 2),
        out_specs=(vmem,) * 3,
        scratch_shapes=scratch,
        compiler_params=pltpu.CompilerParams(collective_id=1, has_side_effects=True, vmem_limit_bytes=VMEM_LIMIT),
    )(*blocks, table, far)


def contract(a, b, on_a, on_b):
    return lax.dot_general(a, b, (((on_a,), (on_b,)), ((), ())), preferred_element_type=F32)


GELU_SCALE = 0.7978845608028654


def expert_kernel(
    chips, both_ref, w_in_ref, w_out_ref, back_ref, keep_ref, leave_ref,
    rows_ref, x_ref, g_ref, act_ref, gpre_ref, part_ref, sib_ref, ret_ref,
    in_sem, fwd_sem, sib_sem, out_sem,
):
    seq, shard = lax.axis_index("seq"), lax.axis_index("shard")
    chip, core = shard // 2, shard % 2
    sibling = (seq, shard + 1 - 2 * core)
    slots, width = both_ref.shape[1] // 2, both_ref.shape[2]
    hidden = w_in_ref.shape[1]

    def device_of(other):
        return (seq, 2 * other + core)

    greet([device_of((chip + j) % chips) for j in range(1, chips)] + [sibling])
    sent = []
    copies = {}
    for j in range(1, chips):
        to = (chip + j) % chips
        copy = pltpu.make_async_remote_copy(
            both_ref.at[to], rows_ref.at[chip, core], in_sem.at[0, j], in_sem.at[1, j],
            device_id=device_of(to), device_id_type=MESH,
        )
        copy.start()
        copies[j] = copy
        sent.append(copy)
    rows_ref[chip, core] = both_ref[chip]
    forwards = []
    for j in range(chips):
        source = (chip + chips - j) % chips
        if j:
            copies[j].wait_recv()
        copy = pltpu.make_async_remote_copy(
            rows_ref.at[source, core], rows_ref.at[source, core], fwd_sem.at[0, j], fwd_sem.at[1, j],
            device_id=sibling, device_id_type=MESH,
        )
        copy.start()
        forwards.append(copy)
        sent.append(copy)
    for copy in forwards:
        copy.wait_recv()

    group = chips
    while group * 2 * slots > 512:
        group //= 2
    block = group * 2 * slots
    piece = 512

    @pl.loop(0, chips // group)
    def _(t):
        rows = rows_ref[pl.ds(t * group, group)].astype(F32)
        x = rows[:, :, :slots].reshape(block, width).astype(BF16)
        g = rows[:, :, slots:].reshape(block, width).astype(BF16)
        out_sum = jnp.zeros((block, width), F32)
        half_sum = jnp.zeros((block, width), F32)
        where = pl.ds(pl.multiple_of(t * block, block), block)
        x_ref[where] = x
        g_ref[where] = g
        for h in range(hidden // piece):
            cols = pl.ds(h * piece, piece)
            pre = jnp.dot(x, w_in_ref[:, cols], preferred_element_type=F32)
            gact = contract(g, w_out_ref[cols, :], 1, 1)
            square = pre * pre
            t_val = jnp.tanh(GELU_SCALE * (pre + 0.044715 * square * pre))
            act = (0.5 * pre * (1.0 + t_val)).astype(BF16)
            slope = 0.5 * (1.0 + t_val) + 0.5 * pre * (1.0 - t_val * t_val) * (
                GELU_SCALE * (1.0 + 0.134145 * square)
            )
            gpre = (gact * slope).astype(BF16)
            act_ref[where, cols] = act
            gpre_ref[where, cols] = gpre
            out_sum += jnp.dot(act, w_out_ref[cols, :], preferred_element_type=F32)
            half_sum += contract(gpre, w_in_ref[:, cols], 1, 1)
        out_sum = out_sum.reshape(group, 2, slots, width)
        half_sum = half_sum.reshape(group, 2, slots, width)
        both = jnp.concatenate([out_sum, half_sum], axis=2).astype(BF16)
        for u in range(2):
            part_ref[u, pl.ds(t * group, group)] = both[:, u]

    swap = pltpu.make_async_remote_copy(
        part_ref.at[1 - core], sib_ref, sib_sem.at[0], sib_sem.at[1], device_id=sibling, device_id_type=MESH
    )
    swap.start()
    sent.append(swap)
    side = hidden // 2
    away = pl.ds(pl.multiple_of((1 - seq) * side, side), side)
    home = pl.ds(pl.multiple_of(seq * side, side), side)
    returns = []
    swap.wait_recv()
    ret_ref[...] = (part_ref[core].astype(F32) + sib_ref[...].astype(F32)).astype(BF16)
    for j in range(1, chips):
        to = (chip + j) % chips
        copy = pltpu.make_async_remote_copy(
            ret_ref.at[to], back_ref.at[chip], out_sem.at[0, j], out_sem.at[1, j],
            device_id=device_of(to), device_id_type=MESH,
        )
        copy.start()
        returns.append(copy)
        sent.append(copy)
    back_ref[chip] = ret_ref[chip]
    for target, cols in ((leave_ref, away), (keep_ref, home)):
        target[0] = contract(x_ref[...], gpre_ref[:, cols], 0, 0).astype(BF16)
        target[1] = contract(act_ref[:, cols], g_ref[...], 0, 0).astype(BF16)
    for copy in returns:
        copy.wait_recv()
    for copy in sent:
        copy.wait_send()


def run_experts(both, w_in, w_out):
    chips, doubled, width = both.shape
    hidden = w_in.shape[1]
    rows = chips * doubled
    vmem = pl.BlockSpec(memory_space=pltpu.VMEM)
    half = jax.ShapeDtypeStruct((2, width, hidden // 2), BF16)
    return pl.pallas_call(
        functools.partial(expert_kernel, chips),
        out_shape=(jax.ShapeDtypeStruct(both.shape, BF16), half, half),
        in_specs=[vmem] * 3,
        out_specs=(vmem,) * 3,
        scratch_shapes=[
            pltpu.VMEM((chips, 2, doubled, width), BF16),
            pltpu.VMEM((rows, width), BF16),
            pltpu.VMEM((rows, width), BF16),
            pltpu.VMEM((rows, hidden), BF16),
            pltpu.VMEM((rows, hidden), BF16),
            pltpu.VMEM((2, chips, doubled, width), BF16),
            pltpu.VMEM((chips, doubled, width), BF16),
            pltpu.VMEM((chips, doubled, width), BF16),
            pltpu.SemaphoreType.DMA((2, chips)),
            pltpu.SemaphoreType.DMA((2, chips)),
            pltpu.SemaphoreType.DMA((2,)),
            pltpu.SemaphoreType.DMA((2, chips)),
        ],
        compiler_params=pltpu.CompilerParams(collective_id=2, has_side_effects=True, vmem_limit_bytes=VMEM_LIMIT),
    )(both, w_in, w_out)


def rms_parts(values):
    inverse = lax.rsqrt(jnp.mean(values * values, axis=-1, keepdims=True) + EPS)
    return (values * inverse, inverse)


def rms_back(grad_normed, normed, inverse):
    return inverse * (grad_normed - normed * jnp.mean(grad_normed * normed, axis=-1, keepdims=True))


def attend_kernel(own_ref, all_ref, wq_ref, wk_ref, wv_ref, offset_ref, q_ref, k_ref, v_ref, probs_ref, mixed_ref):
    own, every = own_ref[...], all_ref[...]
    q_ref[...] = jnp.dot(own, wq_ref[...], preferred_element_type=F32).astype(BF16)
    k_ref[...] = jnp.dot(every, wk_ref[...], preferred_element_type=F32).astype(BF16)
    v_ref[...] = jnp.dot(every, wv_ref[...], preferred_element_type=F32).astype(BF16)
    here, length = own.shape[0], every.shape[0]
    period = offset_ref.shape[1]
    for pair in range(probs_ref.shape[0] // 2):
        cols = pl.ds(2 * HEAD_DIM * pair, 2 * HEAD_DIM)
        q, k, v = q_ref[:, cols], k_ref[:, cols], v_ref[:, cols]
        mixed = []
        for side in range(2):
            head = 2 * pair + side
            part = slice(side * HEAD_DIM, (side + 1) * HEAD_DIM)
            line = jnp.broadcast_to(offset_ref[head : head + 1, :], (here, period))
            bias = pltpu.roll(line, period - here + 1, 1, stride=1, stride_axis=0)[:, :length]
            scores = contract(q[:, part], k[:, part], 1, 1) + bias
            weights = jnp.exp(scores - jnp.max(scores, axis=-1, keepdims=True))
            probs = weights / jnp.sum(weights, axis=-1, keepdims=True)
            probs_ref[head] = probs
            mixed.append(jnp.dot(probs.astype(BF16), v[:, part], preferred_element_type=F32))
        mixed_ref[:, cols] = jnp.concatenate(mixed, axis=1).astype(BF16)


def attend(own, every, wq, wk, wv, per_offset, heads):
    vmem = pl.BlockSpec(memory_space=pltpu.VMEM)
    low_own = jax.ShapeDtypeStruct(own.shape, BF16)
    low_all = jax.ShapeDtypeStruct(every.shape, BF16)
    probs = jax.ShapeDtypeStruct((heads, own.shape[0], every.shape[0]), F32)
    return pl.pallas_call(
        attend_kernel,
        out_shape=(low_own, low_all, low_all, probs, low_own),
        in_specs=[vmem] * 6,
        out_specs=(vmem,) * 5,
        compiler_params=pltpu.CompilerParams(vmem_limit_bytes=VMEM_LIMIT),
    )(own, every, wq, wk, wv, per_offset)


def attend_back_kernel(
    devices, own_ref, all_ref, wq_ref, wk_ref, wv_ref, wo_ref, q_ref, k_ref, v_ref, probs_ref, mixed_ref, branch_ref,
    main_ref, back_own_ref, back_all_ref, offset_ref, gq_ref, gk_ref, gv_ref, gm_ref,
):
    here, length = own_ref.shape[0], all_ref.shape[0]
    width = own_ref.shape[1]
    period = offset_ref.shape[1]
    branch = branch_ref[...]
    gm_ref[...] = contract(branch, wo_ref[...], 1, 1).astype(BF16)
    down = lax.broadcasted_iota(jnp.int32, (here, here), 0)
    across = lax.broadcasted_iota(jnp.int32, (here, here), 1)
    flip = jnp.where(down + across == here - 1, 1.0, 0.0).astype(BF16)
    offset_ref[...] = jnp.zeros_like(offset_ref)
    for pair in range(probs_ref.shape[0] // 2):
        cols = pl.ds(2 * HEAD_DIM * pair, 2 * HEAD_DIM)
        q, k, v, gm = q_ref[:, cols], k_ref[:, cols], v_ref[:, cols], gm_ref[:, cols]
        grads = [[], [], []]
        for side in range(2):
            head = 2 * pair + side
            part = slice(side * HEAD_DIM, (side + 1) * HEAD_DIM)
            probs = probs_ref[head]
            grad_probs = contract(gm[:, part], v[:, part], 1, 1)
            centre = jnp.sum(probs * grad_probs, axis=-1, keepdims=True)
            scores = (probs * (grad_probs - centre)).astype(BF16)
            grads[0].append(jnp.dot(scores, k[:, part], preferred_element_type=F32))
            grads[1].append(contract(scores, q[:, part], 0, 0))
            grads[2].append(contract(probs.astype(BF16), gm[:, part], 0, 0))
            turned = jnp.dot(flip, scores, preferred_element_type=F32)
            turned = jnp.concatenate([turned, jnp.zeros((here, period - length), F32)], axis=1)
            turned = pltpu.roll(turned, 0, 1, stride=1, stride_axis=0)
            offset_ref[head : head + 1, :] = jnp.sum(turned, axis=0, keepdims=True)
        for ref, halves in zip((gq_ref, gk_ref, gv_ref), grads):
            ref[:, cols] = jnp.concatenate(halves, axis=1).astype(BF16)
    gq, gk, gv = gq_ref[...], gk_ref[...], gv_ref[...]
    back_own_ref[...] = contract(gq, wq_ref[...], 1, 1)
    back_all_ref[...] = contract(gk, wk_ref[...], 1, 1) + contract(gv, wv_ref[...], 1, 1)
    pairs = (
        ((own_ref, gq), (all_ref, gk)),
        ((all_ref, gv), (mixed_ref, branch)),
    )
    if main_ref.shape[0] == devices:
        rows = width // devices
        for n, some in enumerate(pairs):
            both = [contract(left[...], right, 0, 0).reshape(devices, rows, width) for left, right in some]
            main_ref[:, pl.ds(2 * rows * n, 2 * rows)] = jnp.concatenate(both, axis=1).astype(BF16)
    else:
        for n, some in enumerate(pairs):
            for m, (left, right) in enumerate(some):
                main_ref[2 * n + m] = contract(left[...], right, 0, 0).astype(BF16)


def attend_back(devices, own, every, wq, wk, wv, wo, q, k, v, probs, mixed, branch, packed):
    vmem = pl.BlockSpec(memory_space=pltpu.VMEM)
    here, width = own.shape
    length = every.shape[0]
    main = (devices, 4 * (width // devices), width) if packed else (4, width, width)
    return pl.pallas_call(
        functools.partial(attend_back_kernel, devices),
        out_shape=(
            jax.ShapeDtypeStruct(main, BF16),
            jax.ShapeDtypeStruct((here, width), F32),
            jax.ShapeDtypeStruct((length, width), F32),
            jax.ShapeDtypeStruct((16, here + length), F32),
        ),
        in_specs=[vmem] * 12,
        out_specs=(vmem,) * 4,
        scratch_shapes=[
            pltpu.VMEM((here, width), BF16),
            pltpu.VMEM((length, width), BF16),
            pltpu.VMEM((length, width), BF16),
            pltpu.VMEM((here, width), BF16),
        ],
        compiler_params=pltpu.CompilerParams(vmem_limit_bytes=VMEM_LIMIT),
    )(own, every, wq, wk, wv, wo, q, k, v, probs, mixed, branch)


def local(
    devices_along_shard, tokens_in, w_query, w_key, w_value, output_weight, gain_attn, gain_moe, router_weight,
    bias_table, w_expert_in, w_expert_out, expert_id, slot_id, bucket_id, cotangent,
):
    bits = devices_along_shard.bit_length() - 1
    devices = 2 * devices_along_shard
    seq = lax.axis_index("seq")
    rows, width = w_query.shape
    experts = router_weight.shape[1]
    tokens_here = tokens_in.shape[1]
    length = 2 * tokens_here
    capacity = 2 * max(1, 5 * tokens_here // (8 * experts))
    slots = round_up(capacity, 8)
    pack_rows = round_up(4 * rows + 1, 16)
    heads_side, buckets = bias_table.shape

    extra = jnp.concatenate([router_weight.reshape(-1), gain_attn, gain_moe])
    extra = jnp.pad(extra, (0, width - extra.shape[0]))[None]
    pack = jnp.concatenate([w_query, w_key, w_value, output_weight, extra], axis=0)
    pack = jnp.pad(pack, ((0, pack_rows - pack.shape[0]), (0, 0)))
    table_tile = jnp.pad(bias_table, ((0, 16 - heads_side), (0, 128 - buckets)))
    gathered, both_tokens, both_tables = gather_all(pack, tokens_in[0], table_tile, bits)
    gathered = gathered.reshape(devices, pack_rows, width)
    full_query, full_key, full_value, full_output = (
        gathered[:, n * rows : (n + 1) * rows].reshape(width, width) for n in range(4)
    )
    extra = gathered[:, 4 * rows]
    cut = rows * experts
    full_router = extra[:, :cut].reshape(width, experts)
    full_gain_attn = extra[:, cut : cut + rows].reshape(width).astype(F32)
    full_gain_moe = extra[:, cut + rows : cut + 2 * rows].reshape(width).astype(F32)
    full_table = both_tables[:, :heads_side, :buckets].reshape(2 * heads_side, buckets)

    def mine(array):
        return lax.dynamic_slice_in_dim(array, seq * tokens_here, tokens_here, 0)

    inputs = tokens_in[0].astype(F32)
    normed_all, _ = rms_parts(both_tokens.reshape(length, width).astype(F32))
    normed_attn, inverse_attn = rms_parts(inputs)
    hidden_all = (normed_all * full_gain_attn).astype(BF16)
    hidden_own = (normed_attn * full_gain_attn).astype(BF16)
    bucket_onehot = (jnp.arange(buckets, dtype=jnp.int32)[:, None] == bucket_id[None, :]).astype(BF16)
    onehot_here = lax.dynamic_slice_in_dim(
        bucket_onehot, tokens_here * (1 - seq), tokens_here + length - 1, 1
    )
    onehot_here = jnp.pad(onehot_here, ((0, 0), (0, 1)))
    heads = 2 * heads_side
    per_offset = jnp.dot(
        jnp.pad(full_table, ((0, 16 - heads), (0, 0))), onehot_here, preferred_element_type=F32
    )
    queries, keys, values, probs, mixed = attend(
        hidden_own, hidden_all, full_query, full_key, full_value, per_offset, heads
    )

    after_attn = inputs + jnp.dot(mixed, full_output, preferred_element_type=F32)
    normed_moe, inverse_moe = rms_parts(after_attn)
    hidden_moe = (normed_moe * full_gain_moe).astype(BF16)
    router_logits = jnp.dot(hidden_moe, full_router, preferred_element_type=F32)
    gate_weights = jnp.exp(router_logits - jnp.max(router_logits, axis=-1, keepdims=True))
    gate_probs = gate_weights / jnp.sum(gate_weights, axis=-1, keepdims=True)
    chosen = (expert_id[0][:, None] == jnp.arange(experts, dtype=jnp.int32)[None, :]).astype(F32)
    picked = jnp.sum(gate_probs * chosen, axis=-1, keepdims=True)
    slot_of = jnp.where(slot_id[0] >= 0, expert_id[0] * slots + slot_id[0], -1)
    dispatch = (slot_of[:, None] == jnp.arange(experts * slots, dtype=jnp.int32)[None, :]).astype(BF16)
    grad_out = cotangent[0].astype(F32)
    scaled = (picked * grad_out).astype(BF16)
    buffer = contract(dispatch, hidden_moe, 0, 0).astype(BF16)
    grad_slots = contract(dispatch, scaled, 0, 0).astype(BF16)
    both = jnp.concatenate(
        [buffer.reshape(experts, slots, width), grad_slots.reshape(experts, slots, width)], axis=1
    )
    returned, kept, leaving = run_experts(both, w_expert_in[0], w_expert_out[0])
    arriving = lax.ppermute(leaving, "seq", [(0, 1), (1, 0)])
    expert_slots, grad_buffer = returned[:, :slots], returned[:, slots:]

    combined = jnp.dot(dispatch, expert_slots.reshape(-1, width), preferred_element_type=F32)
    block_out = after_attn + picked * combined
    grad_picked = jnp.sum(grad_out * combined, axis=-1, keepdims=True)
    grad_gates = chosen * grad_picked
    grad_logits = gate_probs * (grad_gates - jnp.sum(gate_probs * grad_gates, axis=-1, keepdims=True))
    grad_logits = grad_logits.astype(BF16)
    grad_router = contract(hidden_moe, grad_logits, 0, 0)
    grad_hidden_moe = contract(grad_logits, full_router, 1, 1)
    grad_hidden_moe = grad_hidden_moe + jnp.dot(
        dispatch, grad_buffer.reshape(-1, width), preferred_element_type=F32
    )
    grad_gain_moe = jnp.sum(grad_hidden_moe * normed_moe, axis=0)
    grad_mid = grad_out + rms_back(grad_hidden_moe * full_gain_moe, normed_moe, inverse_moe)
    grad_branch = grad_mid.astype(BF16)
    packed = rows % 8 == 0
    main, back_query, back_all, grad_offset = attend_back(
        devices, hidden_own, hidden_all, full_query, full_key, full_value, full_output,
        queries, keys, values, probs, mixed, grad_branch, packed,
    )
    grad_table = jnp.einsum(
        "ho,bo->hb", grad_offset, onehot_here.astype(F32), precision=lax.Precision.HIGHEST
    )
    grad_table = jnp.pad(grad_table, ((0, 0), (0, 128 - buckets)))
    grad_gain_attn = jnp.sum(back_query * normed_attn, axis=0) + jnp.sum(back_all * normed_all, axis=0)
    far = lax.dynamic_slice_in_dim(back_all, (1 - seq) * tokens_here, tokens_here, 0).astype(BF16)

    extra = jnp.concatenate(
        [
            grad_router.reshape(devices, rows * experts),
            grad_gain_attn.reshape(devices, rows),
            grad_gain_moe.reshape(devices, rows),
        ],
        axis=1,
    )
    extra = jnp.pad(extra, ((0, 0), (0, width - extra.shape[1])))[:, None].astype(BF16)
    if packed:
        blocks = [main, jnp.pad(extra, ((0, 0), (0, pack_rows - 4 * rows - 1), (0, 0)))]
    else:
        joined = jnp.concatenate([main[n].reshape(devices, rows, width) for n in range(4)] + [extra], axis=1)
        blocks = [jnp.pad(joined, ((0, 0), (0, pack_rows - joined.shape[1]), (0, 0)))]
    blocks = [block.reshape((2,) * (bits + 1) + block.shape[1:]) for block in blocks]
    total, table_sum, far_sum = reduce_all(blocks, grad_table, far, bits)
    share = total[4 * rows]

    grad_hidden_attn = back_query + mine(back_all) + far_sum.astype(F32)
    grad_tokens = grad_mid + rms_back(grad_hidden_attn * full_gain_attn, normed_attn, inverse_attn)
    expert_sum = kept.astype(F32) + arriving.astype(F32)
    return (
        block_out.astype(BF16)[None],
        grad_tokens[None],
        total[:rows],
        total[rows : 2 * rows],
        total[2 * rows : 3 * rows],
        total[3 * rows : 4 * rows],
        share[cut : cut + rows],
        share[cut + rows : cut + 2 * rows],
        share[:cut].reshape(rows, experts),
        lax.dynamic_slice_in_dim(table_sum[:, :buckets], seq * heads_side, heads_side, 0),
        expert_sum[0][None],
        expert_sum[1][None],
    )


def solution(mesh):
    return jax.shard_map(
        functools.partial(local, mesh.shape["shard"]),
        mesh=mesh,
        in_specs=(
            P("shard", "seq", None),
            P(("seq", "shard"), None),
            P(("seq", "shard"), None),
            P(("seq", "shard"), None),
            P(("seq", "shard"), None),
            P(("seq", "shard")),
            P(("seq", "shard")),
            P(("seq", "shard"), None),
            P("seq", None),
            P("shard", None, None),
            P("shard", None, None),
            P("shard", "seq"),
            P("shard", "seq"),
            P(),
            P("shard", "seq", None),
        ),
        out_specs=(
            P("shard", "seq", None),
            P("shard", "seq", None),
            P(("seq", "shard"), None),
            P(("seq", "shard"), None),
            P(("seq", "shard"), None),
            P(("seq", "shard"), None),
            P(("seq", "shard")),
            P(("seq", "shard")),
            P(("seq", "shard"), None),
            P("seq", None),
            P("shard", None, "seq"),
            P("shard", "seq", None),
        ),
        check_vma=False,
    )
```
